128 devices in a mesh: stream: 8 (over y_lo, z), span: 4 (over y_hi, core), depth: 4 (over x).
Axes of the slice: x: 4, y: 4 (y_hi: 2, y_lo: 2; y = y_hi * 2 + y_lo), z: 4, core: 2. Of those that a mesh axis runs over, the one named last changes fastest.
Arguments:
- fluid_velocity: float32 [256, 128, 512], P('stream', 'depth', 'span'), may hold values from 0.2 to 1.5
- fluid_temp: float32 [256, 128, 512], P('stream', 'depth', 'span'), may hold values from -6 to 6
- solid_temp: float32 [256, 64, 512], P('stream', None, 'span'), may hold values from -6 to 6
- channel_mask: int32 [256, 512], P('stream', 'span'), may hold values 0 or 1
- owner_shift: int32 [512], P('span'), may hold values from 0 to 255
Outputs:
- new_velocity: float32 [256, 128, 512], P('stream', 'depth', 'span')
- new_fluid_temp: float32 [256, 128, 512], P('stream', 'depth', 'span')
- new_solid_temp: float32 [256, 64, 512], P('stream', None, 'span')
- wall_temp: float32 [256, 512], P('stream', ('span', 'depth'))
The draws below stay inside these ranges and needn't reach their ends.
Inputs may be any that keep to these rules, and one draw needn't show every extreme that they name: Wall faces lie at wall-normal cell 0 of the fluid; face (s, w) is owned by copper row (s + owner_shift[w]) mod 256 of column w.
All inputs are finite; a program needn't handle non-finite values. No bound on the sum of `channel_mask` on one device may be relied on, other than what follows from the above.
Results may differ from the reference program's by a relative error of at most 0.000068.
Values sent between devices are 32-bit elements; how exact they have to be, the bound alone decides.
A program may use at most 64 MiB of HBM per device.

```python
import math
import jax
import jax.numpy as jnp

SN = 64
SWEEPS = 6
NS = 256
NN = 128
NW = 512


def place_ends(array, key, low, high):
    longest = array.shape.index(max(array.shape))
    spots = []
    for shift in (0, 1):
        where = [jax.random.randint(jax.random.fold_in(key, axis), (), 0, length) for axis, length in enumerate(array.shape)]
        where[longest] = (where[longest] + shift) % array.shape[longest]
        spots.append(tuple(where))
    return array.at[spots[0]].set(low).at[spots[1]].set(high)


def block_levels(key, extent, split, smallest, top_value):
    def one(position, blocks):
        heights = jax.random.uniform(jax.random.fold_in(jax.random.fold_in(key, 6), position), (blocks,), jnp.float32, smallest / len(split), top_value / len(split))
        return jnp.repeat(jnp.exp(heights), extent[position] // blocks).reshape((-1,) + (1,) * (len(extent) - position - 1))

    gain = one(*split[0])
    for cut in split[1:]:
        gain = gain * one(*cut)
    return gain


def gaussian(stream_key, shape, deviation, most, split=(), kind=jnp.bfloat16):
    result = jax.random.normal(stream_key, shape, jnp.float32) * deviation
    if len(split) > 0:
        result = block_levels(stream_key, shape, split, -0.22, 0.18) * result
    return jnp.clip(result, min=-most, max=most).astype(kind)


def setup_inputs(seed: int = 0) -> dict:
    splits = jax.random.split(jax.random.key(seed), 6)
    return {
        "fluid_velocity": jnp.clip(0.2 + 1.3 * jax.random.uniform(splits[0], (NS, NN, NW), jnp.float32) ** block_levels(splits[0], (NS, NN, NW), ((0, 8), (1, 4), (2, 4)), -0.2, 0.2), 0.2, 1.5),
        "fluid_temp": gaussian(splits[1], (NS, NN, NW), 1.0, 6.0, ((0, 8), (1, 4), (2, 4)), jnp.float32),
        "solid_temp": gaussian(splits[2], (NS, SN, NW), 1.0, 6.0, ((0, 8), (2, 4)), jnp.float32),
        "channel_mask": place_ends((jax.random.randint(splits[3], (NS, NW), 0, 4) < 3).astype(jnp.int32), jax.random.fold_in(splits[3], 1), 0, 1),
        "owner_shift": place_ends(jax.random.randint(splits[4], (NW,), 0, NS), jax.random.fold_in(splits[4], 1), 0, NS - 1).astype(jnp.int32),
    }


VISCOSITY = 0.1
DIFFUSIVITY = 0.15
ADVECTION = 0.2
TRANSFER = 0.5


def roll_columns(plane, offset):
    total = plane.shape[0]
    source = (jnp.arange(total, dtype=jnp.int32)[:, None] + offset[None, :].astype(jnp.int32)) % total
    return jnp.take_along_axis(plane, source, axis=0)


def fluid_field(field, below, velocity, coef):
    lower = jnp.concatenate((below[:, None, :], field[:, :-1, :]), axis=1)
    upper = jnp.concatenate((field[:, 1:, :], field[:, -1:, :]), axis=1)
    ahead = jnp.roll(field, -1, 0)
    behind = jnp.roll(field, 1, 0)
    lap = ahead + behind + jnp.roll(field, -1, 2) + jnp.roll(field, 1, 2) + lower + upper - 6.0 * field
    grad = (ahead - behind) * 0.5
    return field + coef * lap - ADVECTION * velocity * grad


def copper_neighbours(iterate):
    zeros = jnp.zeros_like(iterate[:, :1, :])
    upper = jnp.concatenate((iterate[:, 1:, :], zeros), axis=1)
    lower = jnp.concatenate((iterate[:, :1, :], iterate[:, :-1, :]), axis=1)
    return jnp.roll(iterate, -1, 0) + jnp.roll(iterate, 1, 0) + jnp.roll(iterate, -1, 2) + jnp.roll(iterate, 1, 2) + upper + lower


def reference(fluid_velocity, fluid_temp, solid_temp, channel_mask, owner_shift):
    face_temp = roll_columns(solid_temp[:, 0, :], owner_shift)
    below_temp = jnp.where(channel_mask > 0, face_temp, fluid_temp[:, 0, :])
    new_velocity = fluid_field(fluid_velocity, -fluid_velocity[:, 0, :], fluid_velocity, VISCOSITY)
    new_temp = fluid_field(fluid_temp, below_temp, fluid_velocity, DIFFUSIVITY)
    flux = channel_mask.astype(jnp.float32) * TRANSFER * (new_temp[:, 0, :] - face_temp)
    source = roll_columns(flux, -owner_shift)
    rhs = solid_temp.at[:, 0, :].add(source)
    iterate = solid_temp
    for sweep in range(SWEEPS):
        omega = 1.0 / (1.0 + (6.0 / 7.0) * math.cos(math.pi * (2 * sweep + 1) / (2 * SWEEPS)))
        iterate = iterate + omega * (rhs - (7.0 * iterate - copper_neighbours(iterate))) / 7.0
    wall_temp = roll_columns(iterate[:, 0, :], owner_shift)
    return new_velocity, new_temp, iterate, wall_temp
```

```python
import functools
import math

import jax
import jax.numpy as jnp
from jax import lax
from jax.experimental import pallas as pl
from jax.experimental.pallas import tpu as pltpu
from jax.sharding import PartitionSpec as P

SWEEPS = 6
VISCOSITY = 0.1
DIFFUSIVITY = 0.15
ADVECTION = 0.2
TRANSFER = 0.5

LANES = 128
ROWS = 32
CELLS = 32
LAYERS = 64
EXT = ROWS + 2 * SWEEPS
HALF = ROWS // 2
STRIP = HALF + 2 * SWEEPS
PACK = 21
SOURCE_ROWS = 48

V_UP, V_DOWN, T_UP, T_DOWN = 0, 1, 2, 3
N_UP, N_DOWN = 4, 5
W_UP, W_DOWN = 6, 7
T0_UP, T0_DOWN = 8, 9
C_UP, C_DOWN = 10, 11
E_UP, E_DOWN = 12, 13
S_UP, S_DOWN = 14, 15
GATHER = 16


def weight(sweep):
    return 1.0 / (1.0 + 6.0 / 7.0 * math.cos(math.pi * (2 * sweep + 1) / (2 * SWEEPS)))


def lane_of(shape):
    return lax.broadcasted_iota(jnp.int32, shape, len(shape) - 1)


def sub_of(shape):
    return lax.broadcasted_iota(jnp.int32, shape, len(shape) - 2)


def roll(x, shift, axis=None):
    axis = x.ndim - 1 if axis is None else axis
    if isinstance(shift, int):
        shift = shift % x.shape[axis]
        if shift == 0:
            return x
    return pltpu.roll(x, shift, axis)


def route(plane, amount, wanted):
    total = plane.shape[0]
    amount = amount & (total - 1)
    step = total // 2
    plane = jnp.concatenate((plane, plane[:wanted]), axis=0)
    while step >= 8:
        keep = wanted + step
        bits = jnp.broadcast_to(amount, (keep, LANES)) & step
        plane = jnp.where(bits != 0, plane[step : step + keep], plane[:keep])
        step //= 2
    keep = wanted + 8
    while step >= 1:
        bits = jnp.broadcast_to(amount, (keep, LANES)) & step
        plane = jnp.where(bits != 0, roll(plane, keep - step, 0), plane)
        step //= 2
    return plane[:wanted]


def regions(lane, parts):
    out = parts[7]
    for n in range(6, -1, -1):
        out = jnp.where(lane < 16 * (n + 1), parts[n], out)
    return out


def rows_loop(first, last, unroll, body, carry):
    count = (last - first) // unroll

    def several(n, carry):
        for u in range(unroll):
            carry = body(first + n * unroll + u, carry)
        return carry

    carry = lax.fori_loop(0, count, several, carry)
    for row in range(first + count * unroll, last):
        carry = body(row, carry)
    return carry


def copper_sweep(out, src, rhs, first, last, sweep):
    omega = weight(sweep)
    keep, gain = 1.0 - omega, omega / 7.0
    sub = sub_of((1, 8, LANES))

    def body(row, carry):
        prev, cur = carry
        nxt = src[row + 1]
        side = roll(cur, 1) + roll(cur, LANES - 1)
        up = jnp.concatenate(
            (cur[1:], jnp.where(sub == 7, 0.0, roll(cur[:1], 7, 1))), axis=0
        )
        down = jnp.concatenate(
            (jnp.where(sub == 0, cur[:1], roll(cur[7:], 1, 1)), cur[:7]), axis=0
        )
        near = (prev + nxt) + (up + down) + side
        out[row] = keep * cur + gain * (rhs[row] + near)
        return cur, nxt

    rows_loop(first, last, 2, body, (src[first - 1], src[first]))


def source_sweep(state, source, first, last, sweep):
    omega = weight(sweep)
    keep, gain = 1.0 - omega, omega / 7.0
    sub = sub_of((8, LANES))

    def fed(row):
        return jnp.where(sub == 0, jnp.broadcast_to(source[pl.ds(row, 1), :], (8, LANES)), 0.0)

    if sweep == 0:

        def begin(row, carry):
            state[row] = gain * fed(row)
            return carry

        rows_loop(first, last, 6, begin, 0)
        return

    def body(row, carry):
        prev, cur = carry
        nxt = state[row + 1]
        side = roll(cur, 1) + roll(cur, LANES - 1)
        up = jnp.where(sub == 7, 0.0, roll(cur, 7, 0))
        down = jnp.where(sub == 0, cur, roll(cur, 1, 0))
        near = (prev + nxt) + (up + down) + side
        state[row] = keep * cur + gain * (fed(row) + near)
        return cur, nxt

    rows_loop(first, last, 8, body, (state[first - 1], state[first]))


def with_edges(lane, main, strip, half):
    low, high = (roll(strip, 0), roll(strip, 96)) if half == 0 else (roll(strip, 64), roll(strip, 32))
    return jnp.where(lane < SWEEPS, low, jnp.where(lane >= LANES - SWEEPS, high, main))


def kernel(
    v_in,
    t_in,
    c_in,
    mask_ref,
    shift_ref,
    v_out,
    t_out,
    c_out,
    wall_ref,
    vb,
    tb,
    xn,
    rm,
    xm,
    rs,
    xs,
    oc,
    ov,
    ot,
    n_send,
    n_recv,
    w_send,
    w_recv,
    t0_recv,
    e_send,
    e_recv,
    surface,
    flux,
    face,
    source,
    strip_source,
    gm,
    gs,
    wall_send,
    wall_all,
    below,
    send_sem,
    recv_sem,
    local_sem,
):
    streams, spans, depths = (lax.axis_size(a) for a in ("stream", "span", "depth"))
    i, j, k = (lax.axis_index(a) for a in ("stream", "span", "depth"))
    up_i, down_i = lax.rem(i + 1, streams), lax.rem(i + streams - 1, streams)
    up_j, down_j = lax.rem(j + 1, spans), lax.rem(j + spans - 1, spans)
    up_k, down_k = lax.rem(k + 1, depths), lax.rem(k + depths - 1, depths)
    is_bottom, is_top = k == 0, k == depths - 1
    mesh_id = pl.DeviceIdType.MESH

    def remote(src, dst, index, **where):
        return pltpu.make_async_remote_copy(
            src_ref=src,
            dst_ref=dst,
            send_sem=send_sem.at[index],
            recv_sem=recv_sem.at[index],
            device_id=where,
            device_id_type=mesh_id,
        )

    def local(src, dst, index):
        return pltpu.make_async_copy(src, dst, local_sem.at[index])

    barrier = pltpu.get_barrier_semaphore()
    for m in range(1, streams):
        pl.semaphore_signal(barrier, inc=1, device_id={"stream": lax.rem(i + m, streams)}, device_id_type=mesh_id)
    for other in (up_j, down_j):
        pl.semaphore_signal(barrier, inc=1, device_id={"span": other}, device_id_type=mesh_id)
    for m in range(1, depths):
        pl.semaphore_signal(barrier, inc=1, device_id={"depth": lax.rem(k + m, depths)}, device_id_type=mesh_id)

    load_t = local(t_in, tb.at[pl.ds(CELLS, ROWS * CELLS)], 0)
    load_v = local(v_in, vb.at[pl.ds(CELLS, ROWS * CELLS)], 1)
    load_c = local(c_in, xn.at[pl.ds(SWEEPS * LAYERS, ROWS * LAYERS)], 2)
    load_t.start()
    load_c.start()
    load_v.start()

    lane32 = lane_of((CELLS, LANES))
    load_t.wait()
    n_send[1] = tb[pl.ds(CELLS + CELLS - 1, ROWS, stride=CELLS), :]
    n_send[3] = tb[pl.ds(CELLS, ROWS, stride=CELLS), :]
    load_c.wait()
    surface[i] = xn[pl.ds(SWEEPS * LAYERS, ROWS, stride=LAYERS), :]
    load_v.wait()
    n_send[0] = vb[pl.ds(CELLS + CELLS - 1, ROWS, stride=CELLS), :]
    n_send[2] = vb[pl.ds(CELLS, ROWS, stride=CELLS), :]

    def pack_fluid(row, carry):
        right, left = carry
        at = pl.ds(pl.multiple_of(CELLS + row * CELLS, CELLS), CELLS)
        v, t = vb[at, :], tb[at, :]
        right = jnp.where(lane32 == row, roll(v, row + 1), right)
        right = jnp.where(lane32 == row + ROWS, roll(t, row + 1 + ROWS), right)
        left = jnp.where(lane32 == row, roll(v, row), left)
        left = jnp.where(lane32 == row + ROWS, roll(t, row + ROWS), left)
        return right, left

    zero32 = jnp.zeros((CELLS, LANES), jnp.float32)
    right, left = rows_loop(0, ROWS, 4, pack_fluid, (zero32, zero32))
    w_send[0] = right
    w_send[1] = left

    pl.semaphore_wait(barrier, streams - 1 + 2 + depths - 1)

    surfaces = [
        remote(surface.at[i], surface.at[i], GATHER + m, stream=lax.rem(i + m, streams))
        for m in range(1, streams)
    ]
    fluxes = [
        remote(flux.at[i], flux.at[i], GATHER + streams + m, stream=lax.rem(i + m, streams))
        for m in range(1, streams)
    ]
    walls = [
        remote(wall_send, wall_all.at[i], GATHER + 2 * streams + m, stream=lax.rem(i + m, streams))
        for m in range(1, streams)
    ]
    planes = [
        remote(n_send.at[3], t0_recv.at[0], T0_UP, span=up_j),
        remote(n_send.at[3], t0_recv.at[1], T0_DOWN, span=down_j),
    ]
    last, first = pl.ds(ROWS * CELLS, CELLS), pl.ds(CELLS, CELLS)
    before, after = pl.ds(0, CELLS), pl.ds((ROWS + 1) * CELLS, CELLS)
    t_halos = [
        remote(tb.at[last], tb.at[before], T_UP, stream=up_i),
        remote(tb.at[first], tb.at[after], T_DOWN, stream=down_i),
    ]
    v_halos = [
        remote(vb.at[last], vb.at[before], V_UP, stream=up_i),
        remote(vb.at[first], vb.at[after], V_DOWN, stream=down_i),
    ]
    n_halos = [
        remote(n_send.at[pl.ds(0, 2)], n_recv.at[pl.ds(0, 2)], N_UP, depth=up_k),
        remote(n_send.at[pl.ds(2, 2)], n_recv.at[pl.ds(2, 2)], N_DOWN, depth=down_k),
    ]
    w_halos = [
        remote(w_send.at[0], w_recv.at[0], W_UP, span=up_j),
        remote(w_send.at[1], w_recv.at[1], W_DOWN, span=down_j),
    ]
    wide = SWEEPS * LAYERS
    c_halos = [
        remote(xn.at[pl.ds(ROWS * LAYERS, wide)], xn.at[pl.ds(0, wide)], C_UP, stream=up_i),
        remote(xn.at[pl.ds(wide, wide)], xn.at[pl.ds(wide + ROWS * LAYERS, wide)], C_DOWN, stream=down_i),
    ]
    e_halos = [
        remote(e_send.at[0], e_recv.at[0], E_UP, span=up_j),
        remote(e_send.at[1], e_recv.at[1], E_DOWN, span=down_j),
    ]
    s_halos = [
        remote(source.at[0], source.at[1], S_UP, span=up_j),
        remote(source.at[0], source.at[2], S_DOWN, span=down_j),
    ]
    copies = [
        remote(source.at[0], source.at[0], GATHER + 3 * streams + m, depth=m) for m in range(1, depths)
    ]

    @pl.when(is_bottom)
    def _():
        for c in surfaces + planes:
            c.start()

    for c in t_halos + v_halos + w_halos + n_halos + c_halos:
        c.start()

    def arrange(row, carry):
        base = row * LAYERS
        for r in range(8):
            rm[row, r] = xn[pl.ds(base + r, 8, stride=8), :]
        return carry

    rows_loop(SWEEPS, SWEEPS + ROWS, 2, arrange, 0)

    for c in t_halos:
        c.wait_recv()

    @pl.when(is_bottom)
    def _():
        for c in surfaces + planes:
            c.wait_recv()
        sub = sub_of((ROWS, LANES))
        lane = lane_of((ROWS, LANES))
        face_temp = route(surface[...].reshape(streams * ROWS, LANES), shift_ref[...] + i * ROWS, ROWS)
        t0 = n_send[3]
        t1 = tb[pl.ds(CELLS + 1, ROWS, stride=CELLS), :]
        v0 = n_send[2]
        mask = mask_ref[...]
        behind = jnp.where(sub == 0, jnp.broadcast_to(tb[pl.ds(0, 1), :], (ROWS, LANES)), roll(t0, 1, 0))
        ahead = jnp.where(
            sub == ROWS - 1,
            jnp.broadcast_to(tb[pl.ds((ROWS + 1) * CELLS, 1), :], (ROWS, LANES)),
            roll(t0, ROWS - 1, 0),
        )
        west = jnp.where(lane == 0, roll(t0_recv[0], 1), roll(t0, 1))
        east = jnp.where(lane == LANES - 1, roll(t0_recv[1], LANES - 1), roll(t0, LANES - 1))
        under = jnp.where(mask > 0, face_temp, t0)
        lap = (ahead + behind) + (west + east) + (under + t1) - 6.0 * t0
        grad = (ahead - behind) * 0.5
        new = t0 + DIFFUSIVITY * lap - ADVECTION * v0 * grad
        flux[i] = mask.astype(jnp.float32) * TRANSFER * (new - face_temp)
        for c in fluxes:
            c.start()
        below[0] = -v0
        below[1] = under

    @pl.when(jnp.logical_not(is_bottom))
    def _():
        n_halos[0].wait_recv()
        below[0] = n_recv[0]
        below[1] = n_recv[1]

    @pl.when(is_bottom)
    def _():
        n_halos[0].wait_recv()

    for c in v_halos + w_halos + n_halos[1:]:
        c.wait_recv()

    sub32 = sub_of((CELLS, LANES))
    w_low, w_high = w_recv[0], w_recv[1]

    def fluid(row, carry):
        base = pl.multiple_of(row * CELLS, CELLS)
        here = pl.ds(base + CELLS, CELLS)
        velocity = vb[here, :]
        for field, (ref, out, coef) in enumerate(((vb, ov, VISCOSITY), (tb, ot, DIFFUSIVITY))):
            x = velocity if field == 0 else ref[here, :]
            behind = ref[pl.ds(base, CELLS), :]
            ahead = ref[pl.ds(base + 2 * CELLS, CELLS), :]
            at = row + field * ROWS
            west = jnp.where(lane32 == 0, roll(w_low, LANES - at), roll(x, 1))
            east = jnp.where(lane32 == LANES - 1, roll(w_high, LANES - 1 - at), roll(x, LANES - 1))
            under = jnp.broadcast_to(below[field, pl.ds(row, 1), :], (CELLS, LANES))
            over = jnp.where(is_top, x[CELLS - 1 :], n_recv[2 + field, pl.ds(row, 1), :])
            over = jnp.broadcast_to(over, (CELLS, LANES))
            lower = jnp.where(sub32 == 0, under, roll(x, 1, 0))
            upper = jnp.where(sub32 == CELLS - 1, over, roll(x, CELLS - 1, 0))
            lap = (ahead + behind) + (west + east) + (lower + upper) - 6.0 * x
            grad = (ahead - behind) * 0.5
            out[pl.ds(base, CELLS), :] = x + coef * lap - ADVECTION * velocity * grad
        return carry

    rows_loop(0, ROWS, 2, fluid, 0)
    store_v = local(ov, v_out, 3)
    store_t = local(ot, t_out, 4)
    store_v.start()
    store_t.start()

    for c in c_halos:
        c.wait_recv()
    rows_loop(0, SWEEPS, 2, arrange, 0)
    rows_loop(SWEEPS + ROWS, EXT, 2, arrange, 0)
    lane8 = lane_of((8, 8, LANES))

    for q in range(2):

        def pack_copper(n, carry):
            high, low = carry
            x = rm[1 + q * PACK + n]
            at = SWEEPS * n
            chosen = jnp.logical_and(lane8 >= at, lane8 < at + SWEEPS)
            high = jnp.where(chosen, roll(x, at + SWEEPS), high)
            low = jnp.where(chosen, roll(x, at), low)
            return high, low

        zero8 = jnp.zeros((8, 8, LANES), jnp.float32)
        high, low = rows_loop(0, PACK, 3, pack_copper, (zero8, zero8))
        e_send[0, q] = high
        e_send[1, q] = low
    for c in e_halos:
        c.start()

    def sweep_main(sweep):
        copper_sweep(xm, rm if sweep == 0 else xm, rm, 1 + sweep, EXT - 1 - sweep, sweep)

    sweep_main(0)

    @pl.when(is_bottom)
    def _():
        for c in fluxes:
            c.wait_recv()
        amount = i * ROWS - SWEEPS - shift_ref[...]
        source[0] = route(flux[...].reshape(streams * ROWS, LANES), amount, SOURCE_ROWS)
        for c in copies:
            c.start()

    sweep_main(1)
    sweep_main(2)

    for m in range(1, depths):

        @pl.when(k == m)
        def _():
            copies[m - 1].wait_recv()

    for c in s_halos:
        c.start()

    for sweep in range(3, SWEEPS):
        sweep_main(sweep)

    for c in e_halos:
        c.wait_recv()

    def build(row, carry):
        x0, x1 = rm[row], rm[row + HALF]
        f0 = jnp.maximum(row - 1, 0)
        f1 = jnp.minimum(row + HALF - 1, 2 * PACK - 1)
        q0, q1 = f0 // PACK, f1 // PACK
        p0, p1 = SWEEPS * (f0 - q0 * PACK), SWEEPS * (f1 - q1 * PACK)
        parts = (
            x0,
            roll(x0, 32),
            roll(e_recv[1, q0], lax.rem(LANES + 32 - p0, LANES)),
            roll(e_recv[0, q1], lax.rem(LANES + 58 - p1, LANES)),
            roll(x1, 64),
            roll(x1, 96),
            roll(e_recv[1, q1], lax.rem(LANES + 96 - p1, LANES)),
            roll(e_recv[0, q0], lax.rem(LANES + 122 - p0, LANES)),
        )
        rs[row] = regions(lane8, parts)
        return carry

    lax.fori_loop(0, STRIP, build, 0)
    for sweep in range(SWEEPS):
        copper_sweep(xs, rs if sweep == 0 else xs, rs, 1 + sweep, STRIP - 1 - sweep, sweep)

    for half in range(2):

        def assemble(n, carry):
            done = with_edges(lane8, xm[n + SWEEPS + half * HALF], xs[n + SWEEPS], half)
            base = (n + half * HALF) * LAYERS
            for r in range(8):
                oc[pl.ds(base + r, 8, stride=8), :] = done[r]
            return carry

        rows_loop(0, HALF, 2, assemble, 0)

    for c in s_halos:
        c.wait_recv()
    lane = lane_of((32, LANES))
    low0, low1 = source[0, pl.ds(0, 32), :], source[0, pl.ds(HALF, 32), :]
    strip_source[...] = regions(
        lane,
        (
            low0,
            roll(low0, 32),
            roll(source[2, pl.ds(0, 32), :], 32),
            roll(source[1, pl.ds(HALF, 32), :], 64),
            roll(low1, 64),
            roll(low1, 96),
            roll(source[2, pl.ds(HALF, 32), :], 96),
            source[1, pl.ds(0, 32), :],
        ),
    )
    for sweep in range(SWEEPS):
        source_sweep(gm, source.at[0], 1 + sweep, EXT - 1 - sweep, sweep)
        source_sweep(gs, strip_source, 1 + sweep, STRIP - 1 - sweep, sweep)
    lane1 = lane_of((8, LANES))
    for half in range(2):

        def add(n, carry):
            at = pl.ds(pl.multiple_of((n + half * HALF) * LAYERS, LAYERS), 8)
            oc[at, :] += with_edges(lane1, gm[n + SWEEPS + half * HALF], gs[n + SWEEPS], half)
            return carry

        rows_loop(0, HALF, 8, add, 0)

    columns = LANES // depths
    tiles = ROWS // 8
    new_surface = oc[pl.ds(0, ROWS, stride=LAYERS), :]
    packed = jnp.zeros((8, LANES), jnp.float32)
    width = LANES // tiles
    for t in range(tiles):
        moved = roll(new_surface[8 * t : 8 * t + 8], lax.rem(LANES + width * t - columns * k, LANES))
        packed = jnp.where(lane1 // width == t, moved, packed)
    wall_send[...] = packed
    for c in walls:
        c.start()
    store_c = local(oc, c_out, 5)
    store_c.start()
    wall_all[i] = packed
    shift = roll(jnp.broadcast_to(shift_ref[...], (8, LANES)), lax.rem(LANES - columns * k, LANES))[:1]
    for c in walls:
        c.wait_recv()
    rows = [roll(wall_all[b], LANES - width * t) for b in range(streams) for t in range(tiles)]
    wall_ref[...] = route(jnp.concatenate(rows, axis=0), shift + i * ROWS, ROWS)[:, : wall_ref.shape[1]]

    for c in t_halos + v_halos + w_halos + n_halos + c_halos + e_halos + s_halos + walls:
        c.wait_send()

    @pl.when(is_bottom)
    def _():
        for c in surfaces + planes + fluxes + copies:
            c.wait_send()

    store_v.wait()
    store_t.wait()
    store_c.wait()


def per_device(fluid_velocity, fluid_temp, solid_temp, channel_mask, owner_shift):
    f32 = jnp.float32
    streams, depths = lax.axis_size("stream"), lax.axis_size("depth")
    fluid_rows, copper_rows = ROWS * CELLS, ROWS * LAYERS
    vmem = pl.BlockSpec(memory_space=pltpu.VMEM)
    anywhere = pl.BlockSpec(memory_space=pl.ANY)
    messages = GATHER + 3 * streams + depths
    outs = pl.pallas_call(
        kernel,
        out_shape=(
            jax.ShapeDtypeStruct((fluid_rows, LANES), f32),
            jax.ShapeDtypeStruct((fluid_rows, LANES), f32),
            jax.ShapeDtypeStruct((copper_rows, LANES), f32),
            jax.ShapeDtypeStruct((ROWS, LANES // depths), f32),
        ),
        in_specs=[anywhere, anywhere, anywhere, vmem, vmem],
        out_specs=(anywhere, anywhere, anywhere, vmem),
        scratch_shapes=[
            pltpu.VMEM(((ROWS + 2) * CELLS, LANES), f32),
            pltpu.VMEM(((ROWS + 2) * CELLS, LANES), f32),
            pltpu.VMEM((EXT * LAYERS, LANES), f32),
            pltpu.VMEM((EXT, 8, 8, LANES), f32),
            pltpu.VMEM((EXT, 8, 8, LANES), f32),
            pltpu.VMEM((STRIP, 8, 8, LANES), f32),
            pltpu.VMEM((STRIP, 8, 8, LANES), f32),
            pltpu.VMEM((copper_rows, LANES), f32),
            pltpu.VMEM((fluid_rows, LANES), f32),
            pltpu.VMEM((fluid_rows, LANES), f32),
            pltpu.VMEM((4, ROWS, LANES), f32),
            pltpu.VMEM((4, ROWS, LANES), f32),
            pltpu.VMEM((2, CELLS, LANES), f32),
            pltpu.VMEM((2, CELLS, LANES), f32),
            pltpu.VMEM((2, ROWS, LANES), f32),
            pltpu.VMEM((2, 2, 8, 8, LANES), f32),
            pltpu.VMEM((2, 2, 8, 8, LANES), f32),
            pltpu.VMEM((streams, ROWS, LANES), f32),
            pltpu.VMEM((streams, ROWS, LANES), f32),
            pltpu.VMEM((ROWS, LANES), f32),
            pltpu.VMEM((3, SOURCE_ROWS, LANES), f32),
            pltpu.VMEM((32, LANES), f32),
            pltpu.VMEM((EXT, 8, LANES), f32),
            pltpu.VMEM((STRIP, 8, LANES), f32),
            pltpu.VMEM((8, LANES), f32),
            pltpu.VMEM((streams, 8, LANES), f32),
            pltpu.VMEM((2, ROWS, LANES), f32),
            pltpu.SemaphoreType.DMA((messages,)),
            pltpu.SemaphoreType.DMA((messages,)),
            pltpu.SemaphoreType.DMA((6,)),
        ],
        compiler_params=pltpu.CompilerParams(
            collective_id=0, has_side_effects=True, vmem_limit_bytes=40 * 1024 * 1024
        ),
    )(
        fluid_velocity.reshape(fluid_rows, LANES),
        fluid_temp.reshape(fluid_rows, LANES),
        solid_temp.reshape(copper_rows, LANES),
        channel_mask,
        owner_shift.reshape(1, LANES),
    )
    return (
        outs[0].reshape(fluid_velocity.shape),
        outs[1].reshape(fluid_temp.shape),
        outs[2].reshape(solid_temp.shape),
        outs[3],
    )


def solution(mesh):
    placed = (
        P("stream", "depth", "span"),
        P("stream", "depth", "span"),
        P("stream", None, "span"),
        P("stream", "span"),
        P("span"),
    )
    return jax.shard_map(
        per_device,
        mesh=mesh,
        in_specs=placed,
        out_specs=(
            P("stream", "depth", "span"),
            P("stream", "depth", "span"),
            P("stream", None, "span"),
            P("stream", ("span", "depth")),
        ),
        check_vma=False,
    )
```

```python
import functools
import math

import jax
import jax.numpy as jnp
from jax import lax
from jax.experimental import pallas as pl
from jax.experimental.pallas import tpu as pltpu
from jax.sharding import PartitionSpec as P

SWEEPS = 6
VISCOSITY = 0.1
DIFFUSIVITY = 0.15
ADVECTION = 0.2
TRANSFER = 0.5

LANES = 128
ROWS = 32
CELLS = 32
LAYERS = 64
EXT = ROWS + 2 * SWEEPS
HALF = ROWS // 2
STRIP = HALF + 2 * SWEEPS
PACK = 10
GROUPS = 3
SOURCE_ROWS = 48

V_UP, V_DOWN, T_UP, T_DOWN = 0, 1, 2, 3
N_UP, N_DOWN = 4, 5
W_UP, W_DOWN = 6, 7
T0_UP, T0_DOWN = 8, 9
C_UP, C_DOWN = 10, 11
E_UP, E_DOWN = 12, 13
S_UP, S_DOWN = 14, 15
GATHER = 16


def weight(sweep):
    return 1.0 / (1.0 + 6.0 / 7.0 * math.cos(math.pi * (2 * sweep + 1) / (2 * SWEEPS)))


def lane_of(shape):
    return lax.broadcasted_iota(jnp.int32, shape, len(shape) - 1)


def sub_of(shape):
    return lax.broadcasted_iota(jnp.int32, shape, len(shape) - 2)


def roll(x, shift, axis=None):
    axis = x.ndim - 1 if axis is None else axis
    if isinstance(shift, int):
        shift = shift % x.shape[axis]
        if shift == 0:
            return x
    return pltpu.roll(x, shift, axis)


def route(plane, amount, wanted):
    total = plane.shape[0]
    amount = amount & (total - 1)
    step = total // 2
    plane = jnp.concatenate((plane, plane[:wanted]), axis=0)
    while step >= 8:
        keep = wanted + step
        bits = jnp.broadcast_to(amount, (keep, LANES)) & step
        plane = jnp.where(bits != 0, plane[step : step + keep], plane[:keep])
        step //= 2
    keep = wanted + 8
    while step >= 1:
        bits = jnp.broadcast_to(amount, (keep, LANES)) & step
        plane = jnp.where(bits != 0, roll(plane, keep - step, 0), plane)
        step //= 2
    return plane[:wanted]


def regions(lane, parts):
    out = parts[7]
    for n in range(6, -1, -1):
        out = jnp.where(lane < 16 * (n + 1), parts[n], out)
    return out


def rows_loop(first, last, unroll, body, carry):
    count = (last - first) // unroll

    def several(n, carry):
        for u in range(unroll):
            carry = body(first + n * unroll + u, carry)
        return carry

    carry = lax.fori_loop(0, count, several, carry)
    for row in range(first + count * unroll, last):
        carry = body(row, carry)
    return carry


def copper_sweep(out, src, rhs, first, last, sweep):
    omega = weight(sweep)
    keep, gain = 1.0 - omega, omega / 7.0
    sub = sub_of((1, 8, LANES))

    def body(row, carry):
        prev, cur = carry
        nxt = src[row + 1]
        side = roll(cur, 1) + roll(cur, LANES - 1)
        up = jnp.concatenate(
            (cur[1:], jnp.where(sub == 7, 0.0, roll(cur[:1], 7, 1))), axis=0
        )
        down = jnp.concatenate(
            (jnp.where(sub == 0, cur[:1], roll(cur[7:], 1, 1)), cur[:7]), axis=0
        )
        near = (prev + nxt) + (up + down) + side
        out[row] = keep * cur + gain * (rhs[row] + near)
        return cur, nxt

    rows_loop(first, last, (last - first) // 2, body, (src[first - 1], src[first]))


def edge_index(row):
    n = lax.rem(row + STRIP - SWEEPS, STRIP)
    group = n // PACK
    return group, SWEEPS * (n - group * PACK)


def kernel(
    v_in,
    t_in,
    c_in,
    mask_ref,
    shift_ref,
    v_out,
    t_out,
    c_out,
    wall_ref,
    vb,
    tb,
    xn,
    rm,
    x0,
    x1,
    rs,
    s0,
    s1,
    n_send,
    n_recv,
    w_send,
    w_recv,
    t0_recv,
    e_send,
    e_recv,
    surface,
    flux,
    source,
    fix,
    strip_source,
    wall_send,
    wall_all,
    below,
    send_sem,
    recv_sem,
    local_sem,
):
    streams, spans, depths = (lax.axis_size(a) for a in ("stream", "span", "depth"))
    i, j, k = (lax.axis_index(a) for a in ("stream", "span", "depth"))
    up_i, down_i = lax.rem(i + 1, streams), lax.rem(i + streams - 1, streams)
    up_j, down_j = lax.rem(j + 1, spans), lax.rem(j + spans - 1, spans)
    up_k, down_k = lax.rem(k + 1, depths), lax.rem(k + depths - 1, depths)
    is_bottom, is_top = k == 0, k == depths - 1
    mesh_id = pl.DeviceIdType.MESH

    def remote(src, dst, index, **where):
        return pltpu.make_async_remote_copy(
            src_ref=src,
            dst_ref=dst,
            send_sem=send_sem.at[index],
            recv_sem=recv_sem.at[index],
            device_id=where,
            device_id_type=mesh_id,
        )

    def local(src, dst, index):
        return pltpu.make_async_copy(src, dst, local_sem.at[index])

    barrier = pltpu.get_barrier_semaphore()
    for m in range(1, streams):
        pl.semaphore_signal(barrier, inc=1, device_id={"stream": lax.rem(i + m, streams)}, device_id_type=mesh_id)
    for other in (up_j, down_j):
        pl.semaphore_signal(barrier, inc=1, device_id={"span": other}, device_id_type=mesh_id)
    for m in range(1, depths):
        pl.semaphore_signal(barrier, inc=1, device_id={"depth": lax.rem(k + m, depths)}, device_id_type=mesh_id)

    load_t = local(t_in, tb.at[pl.ds(CELLS, ROWS * CELLS)], 0)
    load_v = local(v_in, vb.at[pl.ds(CELLS, ROWS * CELLS)], 1)
    load_c = local(c_in, xn.at[pl.ds(SWEEPS * LAYERS, ROWS * LAYERS)], 2)
    load_t.start()
    load_c.start()
    load_v.start()

    lane32 = lane_of((CELLS, LANES))
    load_t.wait()
    n_send[1] = tb[pl.ds(CELLS + CELLS - 1, ROWS, stride=CELLS), :]
    n_send[3] = tb[pl.ds(CELLS, ROWS, stride=CELLS), :]
    load_c.wait()
    surface[i] = xn[pl.ds(SWEEPS * LAYERS, ROWS, stride=LAYERS), :]
    load_v.wait()
    n_send[0] = vb[pl.ds(CELLS + CELLS - 1, ROWS, stride=CELLS), :]
    n_send[2] = vb[pl.ds(CELLS, ROWS, stride=CELLS), :]

    def pack_fluid(row, packed):
        at = pl.ds(pl.multiple_of(CELLS + row * CELLS, CELLS), CELLS)
        low = 2 * row
        for ref, place in ((vb, low), (tb, low + 64)):
            chosen = jnp.logical_or(lane32 == place, lane32 == ((place + LANES - 1) & (LANES - 1)))
            packed = jnp.where(chosen, roll(ref[at, :], place), packed)
        return packed

    w_send[...] = rows_loop(0, ROWS, 8, pack_fluid, jnp.zeros((CELLS, LANES), jnp.float32))

    pl.semaphore_wait(barrier, streams - 1 + 2 + depths - 1)

    surfaces = [
        remote(surface.at[i], surface.at[i], GATHER + m, stream=lax.rem(i + m, streams))
        for m in range(1, streams)
    ]
    fluxes = [
        remote(flux.at[i], flux.at[i], GATHER + streams + m, stream=lax.rem(i + m, streams))
        for m in range(1, streams)
    ]
    walls = [
        remote(wall_send, wall_all.at[i], GATHER + 2 * streams + m, stream=lax.rem(i + m, streams))
        for m in range(1, streams)
    ]
    planes = [
        remote(n_send.at[3], t0_recv.at[0], T0_UP, span=up_j),
        remote(n_send.at[3], t0_recv.at[1], T0_DOWN, span=down_j),
    ]
    last, first = pl.ds(ROWS * CELLS, CELLS), pl.ds(CELLS, CELLS)
    before, after = pl.ds(0, CELLS), pl.ds((ROWS + 1) * CELLS, CELLS)
    t_halos = [
        remote(tb.at[last], tb.at[before], T_UP, stream=up_i),
        remote(tb.at[first], tb.at[after], T_DOWN, stream=down_i),
    ]
    v_halos = [
        remote(vb.at[last], vb.at[before], V_UP, stream=up_i),
        remote(vb.at[first], vb.at[after], V_DOWN, stream=down_i),
    ]
    n_halos = [
        remote(n_send.at[pl.ds(0, 2)], n_recv.at[pl.ds(0, 2)], N_UP, depth=up_k),
        remote(n_send.at[pl.ds(2, 2)], n_recv.at[pl.ds(2, 2)], N_DOWN, depth=down_k),
    ]
    w_halos = [
        remote(w_send, w_recv.at[0], W_UP, span=up_j),
        remote(w_send, w_recv.at[1], W_DOWN, span=down_j),
    ]
    wide = SWEEPS * LAYERS
    c_halos = [
        remote(xn.at[pl.ds(ROWS * LAYERS, wide)], xn.at[pl.ds(0, wide)], C_UP, stream=up_i),
        remote(xn.at[pl.ds(wide, wide)], xn.at[pl.ds(wide + ROWS * LAYERS, wide)], C_DOWN, stream=down_i),
    ]
    e_halos = [
        remote(e_send.at[0], e_recv.at[0], E_UP, span=up_j),
        remote(e_send.at[1], e_recv.at[1], E_DOWN, span=down_j),
    ]
    s_halos = [
        remote(source.at[0], source.at[1], S_UP, span=up_j),
        remote(source.at[0], source.at[2], S_DOWN, span=down_j),
    ]
    copies = [
        remote(source.at[0], source.at[0], GATHER + 3 * streams + m, depth=m) for m in range(1, depths)
    ]

    @pl.when(is_bottom)
    def _():
        for c in surfaces + planes:
            c.start()

    for c in t_halos + v_halos + w_halos + n_halos + c_halos:
        c.start()

    def arrange(row, carry):
        base = row * LAYERS
        for r in range(8):
            rm[row, r] = xn[pl.ds(base + r, 8, stride=8), :]
        return carry

    rows_loop(SWEEPS, SWEEPS + ROWS, 4, arrange, 0)

    lane8 = lane_of((8, 8, LANES))
    part = (lane8 & 63) // 16
    outer = jnp.logical_or(lane8 < 32, lane8 >= 96)

    def edges(row, place, carry):
        high, low = carry
        ends = jnp.where(outer, rm[row], roll(rm[row + HALF], 64))
        rs[row] = jnp.where(part == 1, roll(ends, 32), ends)
        chosen = jnp.logical_and((lane8 & 63) >= place, (lane8 & 63) < place + SWEEPS)
        return (
            jnp.where(chosen, roll(ends, place + SWEEPS), high),
            jnp.where(chosen, roll(ends, place), low),
        )

    zero8 = jnp.zeros((8, 8, LANES), jnp.float32)

    def edge_run(first, last, start, carry):
        return rows_loop(first, last, 2, lambda row, c: edges(row, SWEEPS * (row - start), c), carry)

    e_send[0, 0], e_send[1, 0] = edge_run(SWEEPS, SWEEPS + PACK, SWEEPS, (zero8, zero8))
    middle = SWEEPS + PACK
    e_send[0, 1], e_send[1, 1] = edge_run(middle, HALF + SWEEPS, middle, (zero8, zero8))

    for c in t_halos:
        c.wait_recv()

    @pl.when(is_bottom)
    def _():
        for c in surfaces + planes:
            c.wait_recv()
        sub = sub_of((ROWS, LANES))
        lane = lane_of((ROWS, LANES))
        face_temp = route(surface[...].reshape(streams * ROWS, LANES), shift_ref[...] + i * ROWS, ROWS)
        t0 = n_send[3]
        t1 = tb[pl.ds(CELLS + 1, ROWS, stride=CELLS), :]
        v0 = n_send[2]
        mask = mask_ref[...]
        behind = jnp.where(sub == 0, jnp.broadcast_to(tb[pl.ds(0, 1), :], (ROWS, LANES)), roll(t0, 1, 0))
        ahead = jnp.where(
            sub == ROWS - 1,
            jnp.broadcast_to(tb[pl.ds((ROWS + 1) * CELLS, 1), :], (ROWS, LANES)),
            roll(t0, ROWS - 1, 0),
        )
        west = jnp.where(lane == 0, roll(t0_recv[0], 1), roll(t0, 1))
        east = jnp.where(lane == LANES - 1, roll(t0_recv[1], LANES - 1), roll(t0, LANES - 1))
        under = jnp.where(mask > 0, face_temp, t0)
        lap = (ahead + behind) + (west + east) + (under + t1) - 6.0 * t0
        grad = (ahead - behind) * 0.5
        new = t0 + DIFFUSIVITY * lap - ADVECTION * v0 * grad
        flux[i] = mask.astype(jnp.float32) * TRANSFER * (new - face_temp)
        for c in fluxes:
            c.start()
        below[0] = -v0
        below[1] = under

    @pl.when(jnp.logical_not(is_bottom))
    def _():
        n_halos[0].wait_recv()
        below[0] = n_recv[0]
        below[1] = n_recv[1]

    @pl.when(is_bottom)
    def _():
        n_halos[0].wait_recv()

    for c in v_halos + w_halos + n_halos[1:]:
        c.wait_recv()

    sub32 = sub_of((CELLS, LANES))
    w_all = jnp.where((lane32 & 1) == 0, roll(w_recv[0], 1), roll(w_recv[1], LANES - 1))

    def fluid(row, carry):
        base = pl.multiple_of(row * CELLS, CELLS)
        here = pl.ds(base + CELLS, CELLS)
        velocity = vb[here, :]
        for field, (ref, out, coef) in enumerate(((vb, v_out, VISCOSITY), (tb, t_out, DIFFUSIVITY))):
            x = velocity if field == 0 else ref[here, :]
            behind = ref[pl.ds(base, CELLS), :]
            ahead = ref[pl.ds(base + 2 * CELLS, CELLS), :]
            ends = roll(w_all, lax.rem(LANES - 2 * row, LANES) if field == 0 else 64 - 2 * row)
            west = jnp.where(lane32 == 0, ends, roll(x, 1))
            east = jnp.where(lane32 == LANES - 1, ends, roll(x, LANES - 1))
            under = jnp.broadcast_to(below[field, pl.ds(row, 1), :], (CELLS, LANES))
            over = jnp.where(is_top, x[CELLS - 1 :], n_recv[2 + field, pl.ds(row, 1), :])
            over = jnp.broadcast_to(over, (CELLS, LANES))
            lower = jnp.where(sub32 == 0, under, roll(x, 1, 0))
            upper = jnp.where(sub32 == CELLS - 1, over, roll(x, CELLS - 1, 0))
            lap = (ahead + behind) + (west + east) + (lower + upper) - 6.0 * x
            grad = (ahead - behind) * 0.5
            out[pl.ds(base, CELLS), :] = x + coef * lap - ADVECTION * velocity * grad
        return carry

    rows_loop(0, ROWS, 8, fluid, 0)

    for c in c_halos:
        c.wait_recv()
    rows_loop(0, SWEEPS, 6, arrange, 0)
    rows_loop(SWEEPS + ROWS, EXT, 6, arrange, 0)
    carry = edge_run(HALF + SWEEPS, middle + PACK, middle, (e_send[0, 1], e_send[1, 1]))
    e_send[0, 1], e_send[1, 1] = carry
    carry = edge_run(middle + PACK, STRIP, middle + PACK, (zero8, zero8))
    carry = edge_run(0, SWEEPS, middle + PACK - STRIP, carry)
    e_send[0, 2], e_send[1, 2] = carry
    for c in e_halos:
        c.start()

    @pl.when(is_bottom)
    def _():
        for c in fluxes:
            c.wait_recv()
        amount = i * ROWS - SWEEPS - shift_ref[...]
        source[0] = route(flux[...].reshape(streams * ROWS, LANES), amount, SOURCE_ROWS)
        for c in copies:
            c.start()

    def sweep_main(sweep):
        a, b = (x0, x1) if sweep % 2 == 0 else (x1, x0)
        copper_sweep(a, rm if sweep == 0 else b, rm, 1 + sweep, EXT - 1 - sweep, sweep)

    sweep_main(0)
    sweep_main(1)

    for m in range(1, depths):

        @pl.when(k == m)
        def _():
            copies[m - 1].wait_recv()

    for c in s_halos:
        c.start()

    heat = source[0]
    gains = [weight(n) / 7.0 for n in range(2)]
    once = gains[0] * heat
    near = roll(once, 1, 0) + roll(once, SOURCE_ROWS - 1, 0) + roll(once, 1) + roll(once, LANES - 1) + once
    fix[0] = (1.0 - weight(1)) * once + gains[1] * (heat + near)
    fix[1] = gains[1] * once
    top = sub_of((8, LANES)) == 0

    def top_row(ref, row):
        return jnp.where(top, jnp.broadcast_to(ref[pl.ds(row, 1), :], (8, LANES)), 0.0)

    def mend(row, carry):
        rm[row, 0] += top_row(source.at[0], row)
        x1[row, 0] += top_row(fix.at[0], row)
        x1[row, 1] += top_row(fix.at[1], row)
        return carry

    rows_loop(2, EXT - 2, 8, mend, 0)
    for sweep in range(2, SWEEPS):
        sweep_main(sweep)

    for c in e_halos:
        c.wait_recv()

    def build(row, carry):
        group, place = edge_index(row)
        east = roll(e_recv[1, group], lax.rem(LANES + 32 - place, LANES))
        west = roll(e_recv[0, group], 122 - place)
        rs[row] = jnp.where(part == 2, east, jnp.where(part == 3, west, rs[row]))
        return carry

    rows_loop(0, STRIP, 4, build, 0)
    copper_sweep(s0, rs, rs, 1, STRIP - 1, 0)
    for c in s_halos:
        c.wait_recv()
    lane = lane_of((32, LANES))
    low0, low1 = source[0, pl.ds(0, 32), :], source[0, pl.ds(HALF, 32), :]
    strip_source[...] = regions(
        lane,
        (
            low0,
            roll(low0, 32),
            roll(source[2, pl.ds(0, 32), :], 32),
            roll(source[1, pl.ds(HALF, 32), :], 64),
            roll(low1, 64),
            roll(low1, 96),
            roll(source[2, pl.ds(HALF, 32), :], 96),
            source[1, pl.ds(0, 32), :],
        ),
    )

    def mend_strip(row, carry):
        extra = top_row(strip_source, row)
        rs[row, 0] += extra
        s0[row, 0] += gains[0] * extra
        return carry

    rows_loop(1, STRIP - 1, 13, mend_strip, 0)
    for sweep in range(1, SWEEPS):
        a, b = (s0, s1) if sweep % 2 == 0 else (s1, s0)
        copper_sweep(a, b, rs, 1 + sweep, STRIP - 1 - sweep, sweep)

    def merged(lanes, main0, main1, strip):
        high = roll(strip, 96)
        other = roll(jnp.where(lanes < 64, high, strip), 64)
        return tuple(
            jnp.where(lanes < SWEEPS, low, jnp.where(lanes >= LANES - SWEEPS, up, main))
            for low, up, main in ((strip, high, main0), (other, other, main1))
        )

    lane1 = lane_of((8, LANES))

    def assemble(n, carry):
        halves = merged(lane8, x1[n + SWEEPS], x1[n + SWEEPS + HALF], s1[n + SWEEPS])
        for half, done in enumerate(halves):
            base = (n + half * HALF) * LAYERS
            for r in range(8):
                c_out[pl.ds(base + r, 8, stride=8), :] = done[r]
        return carry

    rows_loop(0, HALF, 4, assemble, 0)

    columns = LANES // depths
    tiles = ROWS // 8
    new_surface = c_out[pl.ds(0, ROWS, stride=LAYERS), :]
    packed = jnp.zeros((8, LANES), jnp.float32)
    width = LANES // tiles
    for t in range(tiles):
        moved = roll(new_surface[8 * t : 8 * t + 8], lax.rem(LANES + width * t - columns * k, LANES))
        packed = jnp.where(lane1 // width == t, moved, packed)
    wall_send[...] = packed
    for c in walls:
        c.start()
    wall_all[i] = packed
    shift = roll(jnp.broadcast_to(shift_ref[...], (8, LANES)), lax.rem(LANES - columns * k, LANES))[:1]
    for c in walls:
        c.wait_recv()
    rows = [roll(wall_all[b], LANES - width * t) for b in range(streams) for t in range(tiles)]
    wall_ref[...] = route(jnp.concatenate(rows, axis=0), shift + i * ROWS, ROWS)[:, : wall_ref.shape[1]]

    for c in t_halos + v_halos + w_halos + n_halos + c_halos + e_halos + s_halos + walls:
        c.wait_send()

    @pl.when(is_bottom)
    def _():
        for c in surfaces + planes + fluxes + copies:
            c.wait_send()


def write_out(*refs):
    *sources, semaphores = refs
    count = len(sources) // 2
    copies = [
        pltpu.make_async_copy(sources[n], sources[count + n], semaphores.at[n]) for n in range(count)
    ]
    for c in copies:
        c.start()
    for c in copies:
        c.wait()


def per_device(fluid_velocity, fluid_temp, solid_temp, channel_mask, owner_shift):
    f32 = jnp.float32
    streams, depths = lax.axis_size("stream"), lax.axis_size("depth")
    fluid_rows, copper_rows = ROWS * CELLS, ROWS * LAYERS
    vmem = pl.BlockSpec(memory_space=pltpu.VMEM)
    anywhere = pl.BlockSpec(memory_space=pl.ANY)
    hbm = pl.BlockSpec(memory_space=pltpu.HBM)
    messages = GATHER + 3 * streams + depths
    outs = pl.pallas_call(
        kernel,
        out_shape=(
            jax.ShapeDtypeStruct((fluid_rows, LANES), f32),
            jax.ShapeDtypeStruct((fluid_rows, LANES), f32),
            jax.ShapeDtypeStruct((copper_rows, LANES), f32),
            jax.ShapeDtypeStruct((ROWS, LANES // depths), f32),
        ),
        in_specs=[hbm, hbm, hbm, vmem, vmem],
        out_specs=(vmem, vmem, vmem, vmem),
        scratch_shapes=[
            pltpu.VMEM(((ROWS + 2) * CELLS, LANES), f32),
            pltpu.VMEM(((ROWS + 2) * CELLS, LANES), f32),
            pltpu.VMEM((EXT * LAYERS, LANES), f32),
            *[pltpu.VMEM((EXT, 8, 8, LANES), f32)] * 3,
            *[pltpu.VMEM((STRIP, 8, 8, LANES), f32)] * 3,
            pltpu.VMEM((4, ROWS, LANES), f32),
            pltpu.VMEM((4, ROWS, LANES), f32),
            pltpu.VMEM((CELLS, LANES), f32),
            pltpu.VMEM((2, CELLS, LANES), f32),
            pltpu.VMEM((2, ROWS, LANES), f32),
            pltpu.VMEM((2, GROUPS, 8, 8, LANES), f32),
            pltpu.VMEM((2, GROUPS, 8, 8, LANES), f32),
            pltpu.VMEM((streams, ROWS, LANES), f32),
            pltpu.VMEM((streams, ROWS, LANES), f32),
            pltpu.VMEM((3, SOURCE_ROWS, LANES), f32),
            pltpu.VMEM((2, SOURCE_ROWS, LANES), f32),
            pltpu.VMEM((32, LANES), f32),
            pltpu.VMEM((8, LANES), f32),
            pltpu.VMEM((streams, 8, LANES), f32),
            pltpu.VMEM((2, ROWS, LANES), f32),
            pltpu.SemaphoreType.DMA((messages,)),
            pltpu.SemaphoreType.DMA((messages,)),
            pltpu.SemaphoreType.DMA((3,)),
        ],
        compiler_params=pltpu.CompilerParams(
            collective_id=0, has_side_effects=True, vmem_limit_bytes=24 * 1024 * 1024
        ),
    )(
        fluid_velocity.reshape(fluid_rows, LANES),
        fluid_temp.reshape(fluid_rows, LANES),
        solid_temp.reshape(copper_rows, LANES),
        channel_mask,
        owner_shift.reshape(1, LANES),
    )
    outs = pl.pallas_call(
        write_out,
        out_shape=tuple(jax.ShapeDtypeStruct(o.shape, o.dtype) for o in outs),
        in_specs=[anywhere] * 4,
        out_specs=(anywhere,) * 4,
        scratch_shapes=[pltpu.SemaphoreType.DMA((4,))],
        compiler_params=pltpu.CompilerParams(vmem_limit_bytes=1024 * 1024),
    )(*outs)
    return (
        outs[0].reshape(fluid_velocity.shape),
        outs[1].reshape(fluid_temp.shape),
        outs[2].reshape(solid_temp.shape),
        outs[3],
    )


def solution(mesh):
    placed = (
        P("stream", "depth", "span"),
        P("stream", "depth", "span"),
        P("stream", None, "span"),
        P("stream", "span"),
        P("span"),
    )
    return jax.shard_map(
        per_device,
        mesh=mesh,
        in_specs=placed,
        out_specs=(
            P("stream", "depth", "span"),
            P("stream", "depth", "span"),
            P("stream", None, "span"),
            P("stream", ("span", "depth")),
        ),
        check_vma=False,
    )
```

```python
import math

import jax
import jax.numpy as jnp
from jax import lax
from jax.experimental import pallas as pl
from jax.experimental.pallas import tpu as pltpu
from jax.sharding import PartitionSpec as P

SWEEPS = 6
VISCOSITY = 0.1
DIFFUSIVITY = 0.15
ADVECTION = 0.2
TRANSFER = 0.5

LANES = 128
ROWS = 32
CELLS = 32
LAYERS = 64
EXT = ROWS + 2 * SWEEPS
HALF = ROWS // 2
STRIP = HALF + SWEEPS
PACK = 10
GROUPS = 3
SOURCE_ROWS = 48

V_UP, V_DOWN, T_UP, T_DOWN = 0, 1, 2, 3
N_UP, N_DOWN = 4, 5
W_UP, W_DOWN = 6, 7
T0_UP, T0_DOWN = 8, 9
C_UP, C_DOWN = 10, 11
E_UP, E_DOWN = 12, 13
S_UP, S_DOWN = 14, 15
CORNER = 16
GATHER = 20


def weight(sweep):
    return 1.0 / (1.0 + 6.0 / 7.0 * math.cos(math.pi * (2 * sweep + 1) / (2 * SWEEPS)))


def lane_of(shape):
    return lax.broadcasted_iota(jnp.int32, shape, len(shape) - 1)


def sub_of(shape):
    return lax.broadcasted_iota(jnp.int32, shape, len(shape) - 2)


def roll(x, shift, axis=None):
    axis = x.ndim - 1 if axis is None else axis
    if isinstance(shift, int):
        shift = shift % x.shape[axis]
        if shift == 0:
            return x
    return pltpu.roll(x, shift, axis)


def route(plane, amount, wanted):
    total = plane.shape[0]
    amount = amount & (total - 1)
    step = total // 2
    plane = jnp.concatenate((plane, plane[:wanted]), axis=0)
    while step >= 8:
        keep = wanted + step
        bits = jnp.broadcast_to(amount, (keep, LANES)) & step
        plane = jnp.where(bits != 0, plane[step : step + keep], plane[:keep])
        step //= 2
    keep = wanted + 8
    while step >= 1:
        bits = jnp.broadcast_to(amount, (keep, LANES)) & step
        plane = jnp.where(bits != 0, roll(plane, keep - step, 0), plane)
        step //= 2
    return plane[:wanted]


def regions(lane, parts):
    out = parts[7]
    for n in range(6, -1, -1):
        out = jnp.where(lane < 16 * (n + 1), parts[n], out)
    return out


def rows_loop(first, last, unroll, body, carry):
    count = (last - first) // unroll

    def several(n, carry):
        for u in range(unroll):
            carry = body(first + n * unroll + u, carry)
        return carry

    carry = several(0, carry) if count == 1 else lax.fori_loop(0, count, several, carry)
    for row in range(first + count * unroll, last):
        carry = body(row, carry)
    return carry


def after(src, row, cur, last, mirrored):
    if mirrored and row == last - 1:
        return roll(cur, 64)
    return src[row + 1]


def copper_sweep(out, src, rhs, first, last, sweep, mirrored=False):
    omega = weight(sweep)
    keep, gain = 1.0 - omega, omega / 7.0
    sub = sub_of((1, 8, LANES))

    def body(row, carry):
        prev, cur = carry
        nxt = after(src, row, cur, last, mirrored)
        side = roll(cur, 1) + roll(cur, LANES - 1)
        up = jnp.concatenate(
            (cur[1:], jnp.where(sub == 7, 0.0, roll(cur[:1], 7, 1))), axis=0
        )
        down = jnp.concatenate(
            (jnp.where(sub == 0, cur[:1], roll(cur[7:], 1, 1)), cur[:7]), axis=0
        )
        near = (prev + nxt) + (up + down) + side
        out[row] = keep * cur + gain * (rhs[row] + near)
        return cur, nxt

    unroll = last - first if last - first <= 16 else (last - first) // 2
    rows_loop(first, last, unroll, body, (src[first - 1], src[first]))


def source_row(source, row):
    wide = jnp.broadcast_to(source[pl.ds(row, 1), :], (8, LANES))
    return jnp.where(sub_of((8, LANES)) == 0, wide, 0.0)


def response_sweep(out, src, source, first, last, sweep, mirrored=False):
    omega = weight(sweep)
    keep, gain = 1.0 - omega, omega / 7.0
    sub = sub_of((8, LANES))

    def begin(row, carry):
        out[row] = gain * source_row(source, row)
        return carry

    def body(row, carry):
        prev, cur = carry
        nxt = after(src, row, cur, last, mirrored)
        side = roll(cur, 1) + roll(cur, LANES - 1)
        up = jnp.where(sub == 7, 0.0, roll(cur, 7, 0))
        down = jnp.where(sub == 0, cur, roll(cur, 1, 0))
        near = (prev + nxt) + (up + down) + side
        out[row] = keep * cur + gain * (source_row(source, row) + near)
        return cur, nxt

    if sweep == 0:
        rows_loop(first, last, last - first, begin, 0)
    else:
        rows_loop(first, last, last - first, body, (src[first - 1], src[first]))


def edge_index(row):
    n = jnp.where(row < SWEEPS, 2 * PACK + row, row - SWEEPS)
    group = n // PACK
    return group, SWEEPS * (n - group * PACK)


def kernel(
    v_in,
    t_in,
    c_in,
    mask_in,
    shift_in,
    v_out,
    t_out,
    c_out,
    wall_out,
    vb,
    tb,
    xn,
    rm,
    x0,
    x1,
    rs,
    s0,
    s1,
    n_send,
    n_recv,
    w_send,
    w_recv,
    t0_recv,
    e_send,
    e_recv,
    surface,
    flux,
    source,
    strip_source,
    wall_send,
    wall_all,
    below,
    mask_ref,
    shift_ref,
    corner_send,
    corner_recv,
    ov,
    ot,
    oc,
    wall,
    g0,
    g1,
    h0,
    h1,
    turned,
    surface_new,
    send_sem,
    recv_sem,
    local_sem,
):
    streams, spans, depths = (lax.axis_size(a) for a in ("stream", "span", "depth"))
    i, j, k = (lax.axis_index(a) for a in ("stream", "span", "depth"))
    up_i, down_i = lax.rem(i + 1, streams), lax.rem(i + streams - 1, streams)
    up_j, down_j = lax.rem(j + 1, spans), lax.rem(j + spans - 1, spans)
    up_k, down_k = lax.rem(k + 1, depths), lax.rem(k + depths - 1, depths)
    is_bottom, is_top = k == 0, k == depths - 1
    mesh_id = pl.DeviceIdType.MESH

    def remote(src, dst, index, **where):
        return pltpu.make_async_remote_copy(
            src_ref=src,
            dst_ref=dst,
            send_sem=send_sem.at[index],
            recv_sem=recv_sem.at[index],
            device_id=where,
            device_id_type=mesh_id,
        )

    def local(src, dst, index):
        return pltpu.make_async_copy(src, dst, local_sem.at[index])

    barrier = pltpu.get_barrier_semaphore()
    for m in range(1, streams):
        pl.semaphore_signal(barrier, inc=1, device_id={"stream": lax.rem(i + m, streams)}, device_id_type=mesh_id)
    for other in (up_j, down_j):
        pl.semaphore_signal(barrier, inc=1, device_id={"span": other}, device_id_type=mesh_id)
    for a in (up_i, down_i):
        for b in (up_j, down_j):
            pl.semaphore_signal(barrier, inc=1, device_id={"stream": a, "span": b}, device_id_type=mesh_id)
    for m in range(1, depths):
        pl.semaphore_signal(barrier, inc=1, device_id={"depth": lax.rem(k + m, depths)}, device_id_type=mesh_id)

    load_t = local(t_in, tb.at[pl.ds(CELLS, ROWS * CELLS)], 0)
    load_v = local(v_in, vb.at[pl.ds(CELLS, ROWS * CELLS)], 1)
    load_c = local(c_in, xn.at[pl.ds(SWEEPS * LAYERS, ROWS * LAYERS)], 2)
    load_mask = local(mask_in, mask_ref, 3)
    load_shift = local(shift_in, shift_ref, 4)
    loads = (load_t, load_c, load_v, load_mask, load_shift)
    for c in loads:
        c.start()

    lane32 = lane_of((CELLS, LANES))
    load_t.wait()
    n_send[1] = tb[pl.ds(CELLS + CELLS - 1, ROWS, stride=CELLS), :]
    n_send[3] = tb[pl.ds(CELLS, ROWS, stride=CELLS), :]
    load_c.wait()
    surface[i] = xn[pl.ds(SWEEPS * LAYERS, ROWS, stride=LAYERS), :]
    load_v.wait()
    n_send[0] = vb[pl.ds(CELLS + CELLS - 1, ROWS, stride=CELLS), :]
    n_send[2] = vb[pl.ds(CELLS, ROWS, stride=CELLS), :]
    load_mask.wait()
    load_shift.wait()

    def pack_fluid(row, packed):
        at = pl.ds(pl.multiple_of(CELLS + row * CELLS, CELLS), CELLS)
        low = 2 * row
        for ref, place in ((vb, low), (tb, low + 64)):
            chosen = jnp.logical_or(lane32 == place, lane32 == ((place + LANES - 1) & (LANES - 1)))
            packed = jnp.where(chosen, roll(ref[at, :], place), packed)
        return packed

    w_send[...] = rows_loop(0, ROWS, 8, pack_fluid, jnp.zeros((CELLS, LANES), jnp.float32))

    pl.semaphore_wait(barrier, streams - 1 + 2 + 4 + depths - 1)

    surfaces = [
        remote(surface.at[i], surface.at[i], GATHER + m, stream=lax.rem(i + m, streams))
        for m in range(1, streams)
    ]
    fluxes = [
        remote(flux.at[i], flux.at[i], GATHER + streams + m, stream=lax.rem(i + m, streams))
        for m in range(1, streams)
    ]
    walls = [
        remote(wall_send, wall_all.at[i], GATHER + 2 * streams + m, stream=lax.rem(i + m, streams))
        for m in range(1, streams)
    ]
    planes = [
        remote(n_send.at[3], t0_recv.at[0], T0_UP, span=up_j),
        remote(n_send.at[3], t0_recv.at[1], T0_DOWN, span=down_j),
    ]
    last, first = pl.ds(ROWS * CELLS, CELLS), pl.ds(CELLS, CELLS)
    before, after = pl.ds(0, CELLS), pl.ds((ROWS + 1) * CELLS, CELLS)
    t_halos = [
        remote(tb.at[last], tb.at[before], T_UP, stream=up_i),
        remote(tb.at[first], tb.at[after], T_DOWN, stream=down_i),
    ]
    v_halos = [
        remote(vb.at[last], vb.at[before], V_UP, stream=up_i),
        remote(vb.at[first], vb.at[after], V_DOWN, stream=down_i),
    ]
    n_halos = [
        remote(n_send.at[pl.ds(0, 2)], n_recv.at[pl.ds(0, 2)], N_UP, depth=up_k),
        remote(n_send.at[pl.ds(2, 2)], n_recv.at[pl.ds(2, 2)], N_DOWN, depth=down_k),
    ]
    w_halos = [
        remote(w_send, w_recv.at[0], W_UP, span=up_j),
        remote(w_send, w_recv.at[1], W_DOWN, span=down_j),
    ]
    wide = SWEEPS * LAYERS
    c_halos = [
        remote(xn.at[pl.ds(ROWS * LAYERS, wide)], xn.at[pl.ds(0, wide)], C_UP, stream=up_i),
        remote(xn.at[pl.ds(wide, wide)], xn.at[pl.ds(wide + ROWS * LAYERS, wide)], C_DOWN, stream=down_i),
    ]
    e_halos = [
        remote(e_send.at[0], e_recv.at[0, pl.ds(0, 2)], E_UP, span=up_j),
        remote(e_send.at[1], e_recv.at[1, pl.ds(0, 2)], E_DOWN, span=down_j),
    ]
    corners = [
        remote(corner_send.at[0, 0], corner_recv.at[0], CORNER, stream=up_i, span=up_j),
        remote(corner_send.at[0, 1], corner_recv.at[1], CORNER + 1, stream=down_i, span=up_j),
        remote(corner_send.at[1, 0], corner_recv.at[2], CORNER + 2, stream=up_i, span=down_j),
        remote(corner_send.at[1, 1], corner_recv.at[3], CORNER + 3, stream=down_i, span=down_j),
    ]
    s_halos = [
        remote(source.at[0], source.at[1], S_UP, span=up_j),
        remote(source.at[0], source.at[2], S_DOWN, span=down_j),
    ]
    copies = [
        remote(source.at[0], source.at[0], GATHER + 3 * streams + m, depth=m) for m in range(1, depths)
    ]

    @pl.when(is_bottom)
    def _():
        for c in surfaces + planes:
            c.start()

    for c in t_halos:
        c.start()

    @pl.when(jnp.logical_not(is_bottom))
    def _():
        for c in c_halos:
            c.start()

    for c in v_halos + w_halos + n_halos:
        c.start()

    def arrange(row, carry):
        base = row * LAYERS
        for r in range(8):
            rm[row, r] = xn[pl.ds(base + r, 8, stride=8), :]
        return carry

    rows_loop(SWEEPS, SWEEPS + ROWS, 4, arrange, 0)

    lane8 = lane_of((8, 8, LANES))
    part = (lane8 & 63) // 16
    outer = jnp.logical_or(lane8 < 32, lane8 >= 96)

    def ends_of(row, other):
        return jnp.where(outer, rm[row], roll(rm[other], 64))

    def keep_own(row, ends):
        rs[row] = jnp.where(part == 1, roll(ends, 32), ends)

    def pack(ends, place, carry):
        high, low = carry
        chosen = jnp.logical_and((lane8 & 63) >= place, (lane8 & 63) < place + SWEEPS)
        return (
            jnp.where(chosen, roll(ends, place + SWEEPS), high),
            jnp.where(chosen, roll(ends, place), low),
        )

    zero8 = jnp.zeros((8, 8, LANES), jnp.float32)

    def pack_corner(n, carry):
        return pack(ends_of(ROWS + n, 2 * SWEEPS - 1 - n), SWEEPS * n, carry)

    halves = lane_of((4, 8, LANES)) < 64
    for side, both in enumerate(rows_loop(0, SWEEPS, 3, pack_corner, (zero8, zero8))):
        folded = both.reshape(4, 2, 8, LANES)
        even, odd = folded[:, 0], folded[:, 1]
        corner_send[side, 0] = jnp.where(halves, even, roll(odd, 64))
        corner_send[side, 1] = jnp.where(halves, roll(even, 64), odd)
    for group, count in enumerate((PACK, STRIP - SWEEPS - PACK)):

        def pack_own(n, carry):
            row = SWEEPS + group * PACK + n
            ends = ends_of(row, EXT - 1 - row)
            keep_own(row, ends)
            return pack(ends, SWEEPS * n, carry)

        e_send[0, group], e_send[1, group] = rows_loop(0, count, 2, pack_own, (zero8, zero8))

    @pl.when(jnp.logical_not(is_bottom))
    def _():
        for c in e_halos + corners:
            c.start()


    def sweep_main(sweep, first, last):
        a, b = (x0, x1) if sweep % 2 == 0 else (x1, x0)
        copper_sweep(a, rm if sweep == 0 else b, rm, first, last, sweep)

    def sweep_strip(sweep, first, last, mirrored=False):
        a, b = (s0, s1) if sweep % 2 == 0 else (s1, s0)
        copper_sweep(a, rs if sweep == 0 else b, rs, first, last, sweep, mirrored)

    def sweep_inner(sweep):
        sweep_main(sweep, SWEEPS + 1 + sweep, ROWS + SWEEPS - 1 - sweep)

    for sweep in range(2):
        sweep_inner(sweep)

    for c in t_halos:
        c.wait_recv()

    @pl.when(is_bottom)
    def _():
        for c in surfaces + planes:
            c.wait_recv()
        sub = sub_of((ROWS, LANES))
        lane = lane_of((ROWS, LANES))
        face_temp = route(surface[...].reshape(streams * ROWS, LANES), shift_ref[...] + i * ROWS, ROWS)
        t0 = n_send[3]
        t1 = tb[pl.ds(CELLS + 1, ROWS, stride=CELLS), :]
        v0 = n_send[2]
        mask = mask_ref[...]
        behind = jnp.where(sub == 0, jnp.broadcast_to(tb[pl.ds(0, 1), :], (ROWS, LANES)), roll(t0, 1, 0))
        ahead = jnp.where(
            sub == ROWS - 1,
            jnp.broadcast_to(tb[pl.ds((ROWS + 1) * CELLS, 1), :], (ROWS, LANES)),
            roll(t0, ROWS - 1, 0),
        )
        west = jnp.where(lane == 0, roll(t0_recv[0], 1), roll(t0, 1))
        east = jnp.where(lane == LANES - 1, roll(t0_recv[1], LANES - 1), roll(t0, LANES - 1))
        under = jnp.where(mask > 0, face_temp, t0)
        lap = (ahead + behind) + (west + east) + (under + t1) - 6.0 * t0
        grad = (ahead - behind) * 0.5
        new = t0 + DIFFUSIVITY * lap - ADVECTION * v0 * grad
        flux[i] = mask.astype(jnp.float32) * TRANSFER * (new - face_temp)
        for c in fluxes:
            c.start()
        for c in c_halos + e_halos + corners:
            c.start()
        below[0] = -v0
        below[1] = under

    for sweep in range(2, SWEEPS):
        sweep_inner(sweep)

    n_halos[0].wait_recv()

    @pl.when(jnp.logical_not(is_bottom))
    def _():
        below[0] = n_recv[0]
        below[1] = n_recv[1]

    for c in v_halos + w_halos + n_halos[1:]:
        c.wait_recv()

    sub32 = sub_of((CELLS, LANES))
    w_all = jnp.where((lane32 & 1) == 0, roll(w_recv[0], 1), roll(w_recv[1], LANES - 1))

    def fluid(row, carry):
        base = pl.multiple_of(row * CELLS, CELLS)
        here = pl.ds(base + CELLS, CELLS)
        velocity = vb[here, :]
        for field, (ref, out, coef) in enumerate(((vb, ov, VISCOSITY), (tb, ot, DIFFUSIVITY))):
            x = velocity if field == 0 else ref[here, :]
            behind = ref[pl.ds(base, CELLS), :]
            ahead = ref[pl.ds(base + 2 * CELLS, CELLS), :]
            ends = roll(w_all, lax.rem(LANES - 2 * row, LANES) if field == 0 else 64 - 2 * row)
            west = jnp.where(lane32 == 0, ends, roll(x, 1))
            east = jnp.where(lane32 == LANES - 1, ends, roll(x, LANES - 1))
            under = jnp.broadcast_to(below[field, pl.ds(row, 1), :], (CELLS, LANES))
            over = jnp.where(is_top, x[CELLS - 1 :], n_recv[2 + field, pl.ds(row, 1), :])
            over = jnp.broadcast_to(over, (CELLS, LANES))
            lower = jnp.where(sub32 == 0, under, roll(x, 1, 0))
            upper = jnp.where(sub32 == CELLS - 1, over, roll(x, CELLS - 1, 0))
            lap = (ahead + behind) + (west + east) + (lower + upper) - 6.0 * x
            grad = (ahead - behind) * 0.5
            out[pl.ds(base, CELLS), :] = x + coef * lap - ADVECTION * velocity * grad
        return carry

    rows_loop(0, ROWS, 8, fluid, 0)

    store_v = local(ov, v_out, 5)
    store_t = local(ot, t_out, 6)
    store_v.start()
    store_t.start()

    @pl.when(is_bottom)
    def _():
        for c in fluxes:
            c.wait_recv()
        amount = i * ROWS - SWEEPS - shift_ref[...]
        source[0] = route(flux[...].reshape(streams * ROWS, LANES), amount, SOURCE_ROWS)
        for c in copies + s_halos:
            c.start()

    for c in e_halos:
        c.wait_recv()

    def build(row, carry):
        group, place = edge_index(row)
        east = roll(e_recv[1, group], lax.rem(LANES + 32 - place, LANES))
        west = roll(e_recv[0, group], 122 - place)
        rs[row] = jnp.where(part == 2, east, jnp.where(part == 3, west, rs[row]))
        return carry

    rows_loop(SWEEPS, STRIP, 4, build, 0)
    for sweep in range(SWEEPS):
        sweep_strip(sweep, SWEEPS + 1 + sweep, STRIP, True)

    for c in c_halos:
        c.wait_recv()
    rows_loop(0, SWEEPS, 6, arrange, 0)
    rows_loop(SWEEPS + ROWS, EXT, 6, arrange, 0)

    for c in corners:
        c.wait_recv()
    for side in range(2):
        ups, downs = corner_recv[2 * side], corner_recv[2 * side + 1]
        even = jnp.where(halves, ups, roll(downs, 64))
        odd = jnp.where(halves, roll(ups, 64), downs)
        e_recv[side, 2] = jnp.stack((even, odd), axis=1).reshape(8, 8, LANES)

    def begin_strip(row, carry):
        keep_own(row, ends_of(row, EXT - 1 - row))
        return build(row, carry)

    rows_loop(0, SWEEPS, 6, begin_strip, 0)
    for sweep in range(SWEEPS):
        sweep_main(sweep, 1 + sweep, SWEEPS + 1 + sweep)
        sweep_main(sweep, ROWS + SWEEPS - 1 - sweep, EXT - 1 - sweep)
        sweep_strip(sweep, 1 + sweep, SWEEPS + 1 + sweep)
        if sweep == 3:
            for m in range(1, depths):

                @pl.when(k == m)
                def _():
                    copies[m - 1].wait_recv()
                    for c in s_halos:
                        c.start()


    for sweep in range(SWEEPS):
        a, b = (g0, g1) if sweep % 2 == 0 else (g1, g0)
        response_sweep(a, b, source.at[0], 1 + sweep, EXT - 1 - sweep, sweep)

    def merged(lanes, main0, main1, strip):
        high = roll(strip, 96)
        other = roll(jnp.where(lanes < 64, high, strip), 64)
        return tuple(
            jnp.where(lanes < SWEEPS, low, jnp.where(lanes >= LANES - SWEEPS, up, main))
            for low, up, main in ((strip, high, main0), (other, other, main1))
        )

    lane1 = lane_of((8, LANES))

    for c in s_halos:
        c.wait_recv()

    def turn(row, carry):
        for side in range(3):
            turned[side, pl.ds(row, 1), :] = source[side, pl.ds(EXT - 1 - row, 1), :]
        return carry

    rows_loop(0, STRIP + 2, 6, turn, 0)
    lane = lane_of((STRIP + 2, LANES))
    straight = pl.ds(0, STRIP + 2)
    strip_source[...] = regions(
        lane,
        (
            source[0, straight, :],
            roll(source[0, straight, :], 32),
            roll(source[2, straight, :], 32),
            roll(turned[1], 64),
            roll(turned[0], 64),
            roll(turned[0], 96),
            roll(turned[2], 96),
            source[1, straight, :],
        ),
    )
    for sweep in range(SWEEPS):
        a, b = (h0, h1) if sweep % 2 == 0 else (h1, h0)
        response_sweep(a, b, strip_source, 1 + sweep, STRIP, sweep, True)

    columns = LANES // depths
    tiles = ROWS // 8
    for n in range(HALF):
        low, high, edge = n + SWEEPS, EXT - 1 - SWEEPS - n, n + SWEEPS
        both = merged(lane1, x1[low, 0] + g1[low], x1[high, 0] + g1[high], s1[edge, 0] + h1[edge])
        surface_new[pl.ds(n, 1), :] = both[0][:1]
        surface_new[pl.ds(ROWS - 1 - n, 1), :] = both[1][:1]
    new_surface = surface_new[...]
    packed = jnp.zeros((8, LANES), jnp.float32)
    width = LANES // tiles
    for t in range(tiles):
        moved = roll(new_surface[8 * t : 8 * t + 8], lax.rem(LANES + width * t - columns * k, LANES))
        packed = jnp.where(lane1 // width == t, moved, packed)
    wall_send[...] = packed
    for c in walls:
        c.start()
    wall_all[i] = packed
    shift = roll(jnp.broadcast_to(shift_ref[...], (8, LANES)), lax.rem(LANES - columns * k, LANES))[:1]
    def assemble(n, carry):
        low, high = n, ROWS - 1 - n
        both = merged(lane8, x1[low + SWEEPS], x1[high + SWEEPS], s1[n + SWEEPS])
        for row, done in zip((low, high), both):
            for r in range(8):
                oc[pl.ds(row * LAYERS + r, 8, stride=8), :] = done[r]
        return carry

    rows_loop(0, HALF, 4, assemble, 0)
    def add(n, carry):
        low, high = n, ROWS - 1 - n
        both = merged(lane1, g1[low + SWEEPS], g1[high + SWEEPS], h1[n + SWEEPS])
        for row, more in zip((low, high), both):
            oc[pl.ds(pl.multiple_of(row * LAYERS, LAYERS), 8), :] += more
        return carry

    rows_loop(0, HALF, 8, add, 0)
    store_c = local(oc, c_out, 7)
    store_c.start()
    for c in walls:
        c.wait_recv()
    rows = [roll(wall_all[b], LANES - width * t) for b in range(streams) for t in range(tiles)]
    wall[...] = route(jnp.concatenate(rows, axis=0), shift + i * ROWS, ROWS)[:, :columns]
    store_wall = local(wall, wall_out, 8)
    store_wall.start()

    for c in t_halos + v_halos + w_halos + n_halos + c_halos + e_halos + corners + s_halos + walls:
        c.wait_send()

    @pl.when(is_bottom)
    def _():
        for c in surfaces + planes + fluxes + copies:
            c.wait_send()

    for c in (store_v, store_t, store_c, store_wall):
        c.wait()


def write_out(*refs):
    sources, results, stages = refs[:4], refs[4:8], refs[8:12]
    semaphores = refs[12]
    steps = []
    for source, result, stage in zip(sources, results, stages):
        rows = source.shape[0]
        parts = max(1, rows // 512)
        for part in range(parts):
            at = pl.ds(part * (rows // parts), rows // parts)
            read, write = semaphores.at[2 * len(steps)], semaphores.at[2 * len(steps) + 1]
            steps.append(
                (
                    pltpu.make_async_copy(source.at[at], stage.at[at], read),
                    pltpu.make_async_copy(stage.at[at], result.at[at], write),
                )
            )
    for read, _ in steps:
        read.start()
    for read, write in steps:
        read.wait()
        write.start()
    for _, write in steps:
        write.wait()


def per_device(fluid_velocity, fluid_temp, solid_temp, channel_mask, owner_shift):
    f32 = jnp.float32
    streams, depths = lax.axis_size("stream"), lax.axis_size("depth")
    fluid_rows, copper_rows = ROWS * CELLS, ROWS * LAYERS
    anywhere = pl.BlockSpec(memory_space=pl.ANY)
    messages = GATHER + 3 * streams + depths
    outs = pl.pallas_call(
        kernel,
        out_shape=(
            jax.ShapeDtypeStruct((fluid_rows, LANES), f32),
            jax.ShapeDtypeStruct((fluid_rows, LANES), f32),
            jax.ShapeDtypeStruct((copper_rows, LANES), f32),
            jax.ShapeDtypeStruct((ROWS, LANES // depths), f32),
        ),
        in_specs=[anywhere] * 5,
        out_specs=(anywhere,) * 4,
        scratch_shapes=[
            pltpu.VMEM(((ROWS + 2) * CELLS, LANES), f32),
            pltpu.VMEM(((ROWS + 2) * CELLS, LANES), f32),
            pltpu.VMEM((EXT * LAYERS, LANES), f32),
            *[pltpu.VMEM((EXT, 8, 8, LANES), f32)] * 3,
            *[pltpu.VMEM((STRIP, 8, 8, LANES), f32)] * 3,
            pltpu.VMEM((4, ROWS, LANES), f32),
            pltpu.VMEM((4, ROWS, LANES), f32),
            pltpu.VMEM((CELLS, LANES), f32),
            pltpu.VMEM((2, CELLS, LANES), f32),
            pltpu.VMEM((2, ROWS, LANES), f32),
            pltpu.VMEM((2, GROUPS - 1, 8, 8, LANES), f32),
            pltpu.VMEM((2, GROUPS, 8, 8, LANES), f32),
            pltpu.VMEM((streams, ROWS, LANES), f32),
            pltpu.VMEM((streams, ROWS, LANES), f32),
            pltpu.VMEM((3, SOURCE_ROWS, LANES), f32),
            pltpu.VMEM((STRIP + 2, LANES), f32),
            pltpu.VMEM((8, LANES), f32),
            pltpu.VMEM((streams, 8, LANES), f32),
            pltpu.VMEM((2, ROWS, LANES), f32),
            pltpu.VMEM((ROWS, LANES), jnp.int32),
            pltpu.VMEM((1, LANES), jnp.int32),
            pltpu.VMEM((2, 2, 4, 8, LANES), f32),
            pltpu.VMEM((4, 4, 8, LANES), f32),
            pltpu.VMEM((fluid_rows, LANES), f32),
            pltpu.VMEM((fluid_rows, LANES), f32),
            pltpu.VMEM((copper_rows, LANES), f32),
            pltpu.VMEM((ROWS, LANES // depths), f32),
            *[pltpu.VMEM((EXT, 8, LANES), f32)] * 2,
            *[pltpu.VMEM((STRIP, 8, LANES), f32)] * 2,
            pltpu.VMEM((3, STRIP + 2, LANES), f32),
            pltpu.VMEM((ROWS, LANES), f32),
            pltpu.SemaphoreType.DMA((messages,)),
            pltpu.SemaphoreType.DMA((messages,)),
            pltpu.SemaphoreType.DMA((9,)),
        ],
        compiler_params=pltpu.CompilerParams(
            collective_id=0, has_side_effects=True, vmem_limit_bytes=57 * 1024 * 1024
        ),
    )(
        fluid_velocity.reshape(fluid_rows, LANES),
        fluid_temp.reshape(fluid_rows, LANES),
        solid_temp.reshape(copper_rows, LANES),
        channel_mask,
        owner_shift.reshape(1, LANES),
    )
    outs = pl.pallas_call(
        write_out,
        out_shape=tuple(jax.ShapeDtypeStruct(o.shape, o.dtype) for o in outs),
        in_specs=[anywhere] * 4,
        out_specs=(anywhere,) * 4,
        scratch_shapes=[pltpu.VMEM(o.shape, o.dtype) for o in outs] + [pltpu.SemaphoreType.DMA((20,))],
        compiler_params=pltpu.CompilerParams(vmem_limit_bytes=57 * 1024 * 1024),
    )(*outs)
    return (
        outs[0].reshape(fluid_velocity.shape),
        outs[1].reshape(fluid_temp.shape),
        outs[2].reshape(solid_temp.shape),
        outs[3],
    )


def solution(mesh):
    placed = (
        P("stream", "depth", "span"),
        P("stream", "depth", "span"),
        P("stream", None, "span"),
        P("stream", "span"),
        P("span"),
    )
    return jax.shard_map(
        per_device,
        mesh=mesh,
        in_specs=placed,
        out_specs=(
            P("stream", "depth", "span"),
            P("stream", "depth", "span"),
            P("stream", None, "span"),
            P("stream", ("span", "depth")),
        ),
        check_vma=False,
    )
```

```python
import math

import jax
import jax.numpy as jnp
from jax import lax
from jax.experimental import pallas as pl
from jax.experimental.pallas import tpu as pltpu
from jax.sharding import PartitionSpec as P

SWEEPS = 6
VISCOSITY = 0.1
DIFFUSIVITY = 0.15
ADVECTION = 0.2
TRANSFER = 0.5

LANES = 128
ROWS = 32
CELLS = 32
LAYERS = 64
EXT = ROWS + 2 * SWEEPS
HALF = ROWS // 2
STRIP = HALF + SWEEPS
PACK = 10
GROUPS = 3
SOURCE_ROWS = 48

V_UP, V_DOWN, T_UP, T_DOWN = 0, 1, 2, 3
N_UP, N_DOWN = 4, 5
W_UP, W_DOWN = 6, 7
T0_UP, T0_DOWN = 8, 9
C_UP, C_DOWN = 10, 11
E_UP, E_DOWN = 12, 13
S_UP, S_DOWN = 14, 15
CORNER = 16
GATHER = 20


def weight(sweep):
    return 1.0 / (1.0 + 6.0 / 7.0 * math.cos(math.pi * (2 * sweep + 1) / (2 * SWEEPS)))


def lane_of(shape):
    return lax.broadcasted_iota(jnp.int32, shape, len(shape) - 1)


def sub_of(shape):
    return lax.broadcasted_iota(jnp.int32, shape, len(shape) - 2)


def roll(x, shift, axis=None):
    axis = x.ndim - 1 if axis is None else axis
    if isinstance(shift, int):
        shift = shift % x.shape[axis]
        if shift == 0:
            return x
    return pltpu.roll(x, shift, axis)


def route(plane, amount, wanted):
    total = plane.shape[0]
    amount = amount & (total - 1)
    step = total // 2
    plane = jnp.concatenate((plane, plane[:wanted]), axis=0)
    while step >= 8:
        keep = wanted + step
        bits = jnp.broadcast_to(amount, (keep, LANES)) & step
        plane = jnp.where(bits != 0, plane[step : step + keep], plane[:keep])
        step //= 2
    keep = wanted + 8
    while step >= 1:
        bits = jnp.broadcast_to(amount, (keep, LANES)) & step
        plane = jnp.where(bits != 0, roll(plane, keep - step, 0), plane)
        step //= 2
    return plane[:wanted]


def regions(lane, parts):
    out = parts[7]
    for n in range(6, -1, -1):
        out = jnp.where(lane < 16 * (n + 1), parts[n], out)
    return out


def rows_loop(first, last, unroll, body, carry):
    count = (last - first) // unroll

    def several(n, carry):
        for u in range(unroll):
            carry = body(first + n * unroll + u, carry)
        return carry

    carry = several(0, carry) if count == 1 else lax.fori_loop(0, count, several, carry)
    for row in range(first + count * unroll, last):
        carry = body(row, carry)
    return carry


def after(src, row, cur, last, mirrored):
    if mirrored and row == last - 1:
        return roll(cur, 64)
    return src[row + 1]


def copper_sweep(out, src, rhs, first, last, sweep, mirrored=False):
    omega = weight(sweep)
    keep, gain = 1.0 - omega, omega / 7.0
    sub = sub_of((1, 8, LANES))

    def body(row, carry):
        prev, cur = carry
        nxt = after(src, row, cur, last, mirrored)
        side = roll(cur, 1) + roll(cur, LANES - 1)
        up = jnp.concatenate(
            (cur[1:], jnp.where(sub == 7, 0.0, roll(cur[:1], 7, 1))), axis=0
        )
        down = jnp.concatenate(
            (jnp.where(sub == 0, cur[:1], roll(cur[7:], 1, 1)), cur[:7]), axis=0
        )
        near = (prev + nxt) + (up + down) + side
        out[row] = keep * cur + gain * (rhs[row] + near)
        return cur, nxt

    unroll = last - first if last - first <= 16 else (last - first) // 2
    rows_loop(first, last, unroll, body, (src[first - 1], src[first]))


def response(source):
    layers = [weight(0) / 7.0 * source]
    rows = source.shape[0]
    for sweep in range(1, SWEEPS):
        omega = weight(sweep)
        keep, gain = 1.0 - omega, omega / 7.0
        new = []
        for n in range(sweep + 1):
            if n == sweep:
                new.append(gain * layers[n - 1])
                continue
            cur = layers[n]
            near = (roll(cur, 1, 0) + roll(cur, rows - 1, 0)) + (roll(cur, 1) + roll(cur, LANES - 1))
            near += layers[n - 1] if n > 0 else cur + source
            if n + 1 < sweep:
                near += layers[n + 1]
            new.append(keep * cur + gain * near)
        layers = new
    return layers


def with_edges(main, strip):
    lane = lane_of(main.shape)
    first, second = strip[:HALF], strip[HALF:]
    low = jnp.concatenate((first, roll(second, 64)), axis=0)
    high = jnp.concatenate((roll(first, 96), roll(second, 32)), axis=0)
    return jnp.where(lane < SWEEPS, low, jnp.where(lane >= LANES - SWEEPS, high, main))


def edge_index(row):
    n = jnp.where(row < SWEEPS, 2 * PACK + row, row - SWEEPS)
    group = n // PACK
    return group, SWEEPS * (n - group * PACK)


def kernel(
    v_in,
    t_in,
    c_in,
    mask_in,
    shift_in,
    v_out,
    t_out,
    c_out,
    wall_out,
    vb,
    tb,
    xn,
    rm,
    x0,
    x1,
    rs,
    s0,
    s1,
    n_send,
    n_recv,
    w_send,
    w_recv,
    t0_recv,
    e_send,
    e_recv,
    surface,
    flux,
    source,
    wall_send,
    wall_all,
    below,
    mask_ref,
    shift_ref,
    corner_send,
    corner_recv,
    ov,
    ot,
    oc,
    wall,
    main_part,
    strip_part,
    strip_turned,
    turned,
    main_top,
    strip_top,
    send_sem,
    recv_sem,
    local_sem,
):
    streams, spans, depths = (lax.axis_size(a) for a in ("stream", "span", "depth"))
    i, j, k = (lax.axis_index(a) for a in ("stream", "span", "depth"))
    up_i, down_i = lax.rem(i + 1, streams), lax.rem(i + streams - 1, streams)
    up_j, down_j = lax.rem(j + 1, spans), lax.rem(j + spans - 1, spans)
    up_k, down_k = lax.rem(k + 1, depths), lax.rem(k + depths - 1, depths)
    is_bottom, is_top = k == 0, k == depths - 1
    mesh_id = pl.DeviceIdType.MESH

    def remote(src, dst, index, **where):
        return pltpu.make_async_remote_copy(
            src_ref=src,
            dst_ref=dst,
            send_sem=send_sem.at[index],
            recv_sem=recv_sem.at[index],
            device_id=where,
            device_id_type=mesh_id,
        )

    def local(src, dst, index):
        return pltpu.make_async_copy(src, dst, local_sem.at[index])

    barrier = pltpu.get_barrier_semaphore()
    for m in range(1, streams):
        pl.semaphore_signal(barrier, inc=1, device_id={"stream": lax.rem(i + m, streams)}, device_id_type=mesh_id)
    for other in (up_j, down_j):
        pl.semaphore_signal(barrier, inc=1, device_id={"span": other}, device_id_type=mesh_id)
    for a in (up_i, down_i):
        for b in (up_j, down_j):
            pl.semaphore_signal(barrier, inc=1, device_id={"stream": a, "span": b}, device_id_type=mesh_id)
    for m in range(1, depths):
        pl.semaphore_signal(barrier, inc=1, device_id={"depth": lax.rem(k + m, depths)}, device_id_type=mesh_id)

    load_t = local(t_in, tb.at[pl.ds(CELLS, ROWS * CELLS)], 0)
    load_v = local(v_in, vb.at[pl.ds(CELLS, ROWS * CELLS)], 1)
    load_c = local(c_in, xn.at[pl.ds(SWEEPS * LAYERS, ROWS * LAYERS)], 2)
    load_mask = local(mask_in, mask_ref, 3)
    load_shift = local(shift_in, shift_ref, 4)
    loads = (load_t, load_c, load_v, load_mask, load_shift)
    for c in loads:
        c.start()

    lane32 = lane_of((CELLS, LANES))
    load_t.wait()
    n_send[1] = tb[pl.ds(CELLS + CELLS - 1, ROWS, stride=CELLS), :]
    n_send[3] = tb[pl.ds(CELLS, ROWS, stride=CELLS), :]
    load_c.wait()
    surface[i] = xn[pl.ds(SWEEPS * LAYERS, ROWS, stride=LAYERS), :]
    load_v.wait()
    n_send[0] = vb[pl.ds(CELLS + CELLS - 1, ROWS, stride=CELLS), :]
    n_send[2] = vb[pl.ds(CELLS, ROWS, stride=CELLS), :]
    load_mask.wait()
    load_shift.wait()

    def pack_fluid(row, packed):
        at = pl.ds(pl.multiple_of(CELLS + row * CELLS, CELLS), CELLS)
        low = 2 * row
        for ref, place in ((vb, low), (tb, low + 64)):
            chosen = jnp.logical_or(lane32 == place, lane32 == ((place + LANES - 1) & (LANES - 1)))
            packed = jnp.where(chosen, roll(ref[at, :], place), packed)
        return packed

    w_send[...] = rows_loop(0, ROWS, 8, pack_fluid, jnp.zeros((CELLS, LANES), jnp.float32))

    pl.semaphore_wait(barrier, streams - 1 + 2 + 4 + depths - 1)

    surfaces = [
        remote(surface.at[i], surface.at[i], GATHER + m, stream=lax.rem(i + m, streams))
        for m in range(1, streams)
    ]
    fluxes = [
        remote(flux.at[i], flux.at[i], GATHER + streams + m, stream=lax.rem(i + m, streams))
        for m in range(1, streams)
    ]
    walls = [
        remote(wall_send, wall_all.at[i], GATHER + 2 * streams + m, stream=lax.rem(i + m, streams))
        for m in range(1, streams)
    ]
    planes = [
        remote(n_send.at[3], t0_recv.at[0], T0_UP, span=up_j),
        remote(n_send.at[3], t0_recv.at[1], T0_DOWN, span=down_j),
    ]
    last, first = pl.ds(ROWS * CELLS, CELLS), pl.ds(CELLS, CELLS)
    before, after = pl.ds(0, CELLS), pl.ds((ROWS + 1) * CELLS, CELLS)
    t_halos = [
        remote(tb.at[last], tb.at[before], T_UP, stream=up_i),
        remote(tb.at[first], tb.at[after], T_DOWN, stream=down_i),
    ]
    v_halos = [
        remote(vb.at[last], vb.at[before], V_UP, stream=up_i),
        remote(vb.at[first], vb.at[after], V_DOWN, stream=down_i),
    ]
    n_halos = [
        remote(n_send.at[pl.ds(0, 2)], n_recv.at[pl.ds(0, 2)], N_UP, depth=up_k),
        remote(n_send.at[pl.ds(2, 2)], n_recv.at[pl.ds(2, 2)], N_DOWN, depth=down_k),
    ]
    w_halos = [
        remote(w_send, w_recv.at[0], W_UP, span=up_j),
        remote(w_send, w_recv.at[1], W_DOWN, span=down_j),
    ]
    wide = SWEEPS * LAYERS
    c_halos = [
        remote(xn.at[pl.ds(ROWS * LAYERS, wide)], xn.at[pl.ds(0, wide)], C_UP, stream=up_i),
        remote(xn.at[pl.ds(wide, wide)], xn.at[pl.ds(wide + ROWS * LAYERS, wide)], C_DOWN, stream=down_i),
    ]
    e_halos = [
        remote(e_send.at[0], e_recv.at[0, pl.ds(0, 2)], E_UP, span=up_j),
        remote(e_send.at[1], e_recv.at[1, pl.ds(0, 2)], E_DOWN, span=down_j),
    ]
    corners = [
        remote(corner_send.at[0, 0], corner_recv.at[0], CORNER, stream=up_i, span=up_j),
        remote(corner_send.at[0, 1], corner_recv.at[1], CORNER + 1, stream=down_i, span=up_j),
        remote(corner_send.at[1, 0], corner_recv.at[2], CORNER + 2, stream=up_i, span=down_j),
        remote(corner_send.at[1, 1], corner_recv.at[3], CORNER + 3, stream=down_i, span=down_j),
    ]
    s_halos = [
        remote(source.at[0], source.at[1], S_UP, span=up_j),
        remote(source.at[0], source.at[2], S_DOWN, span=down_j),
    ]
    copies = [
        remote(source.at[0], source.at[0], GATHER + 3 * streams + m, depth=m) for m in range(1, depths)
    ]

    @pl.when(is_bottom)
    def _():
        for c in surfaces + planes:
            c.start()

    for c in t_halos:
        c.start()

    @pl.when(jnp.logical_not(is_bottom))
    def _():
        for c in c_halos:
            c.start()

    for c in v_halos + w_halos + n_halos:
        c.start()

    def arrange(row, carry):
        base = row * LAYERS
        for r in range(8):
            rm[row, r] = xn[pl.ds(base + r, 8, stride=8), :]
        return carry

    rows_loop(SWEEPS, SWEEPS + ROWS, 4, arrange, 0)

    lane8 = lane_of((8, 8, LANES))
    part = (lane8 & 63) // 16
    outer = jnp.logical_or(lane8 < 32, lane8 >= 96)

    def ends_of(row, other):
        return jnp.where(outer, rm[row], roll(rm[other], 64))

    def keep_own(row, ends):
        rs[row] = jnp.where(part == 1, roll(ends, 32), ends)

    def pack(ends, place, carry):
        high, low = carry
        chosen = jnp.logical_and((lane8 & 63) >= place, (lane8 & 63) < place + SWEEPS)
        return (
            jnp.where(chosen, roll(ends, place + SWEEPS), high),
            jnp.where(chosen, roll(ends, place), low),
        )

    zero8 = jnp.zeros((8, 8, LANES), jnp.float32)

    def pack_corner(n, carry):
        return pack(ends_of(ROWS + n, 2 * SWEEPS - 1 - n), SWEEPS * n, carry)

    halves = lane_of((4, 8, LANES)) < 64
    for side, both in enumerate(rows_loop(0, SWEEPS, 3, pack_corner, (zero8, zero8))):
        folded = both.reshape(4, 2, 8, LANES)
        even, odd = folded[:, 0], folded[:, 1]
        corner_send[side, 0] = jnp.where(halves, even, roll(odd, 64))
        corner_send[side, 1] = jnp.where(halves, roll(even, 64), odd)
    for group, count in enumerate((PACK, STRIP - SWEEPS - PACK)):

        def pack_own(n, carry):
            row = SWEEPS + group * PACK + n
            ends = ends_of(row, EXT - 1 - row)
            keep_own(row, ends)
            return pack(ends, SWEEPS * n, carry)

        e_send[0, group], e_send[1, group] = rows_loop(0, count, 2, pack_own, (zero8, zero8))

    for c in e_halos + corners:
        c.start()


    def sweep_main(sweep, first, last):
        a, b = (x0, x1) if sweep % 2 == 0 else (x1, x0)
        copper_sweep(a, rm if sweep == 0 else b, rm, first, last, sweep)

    def sweep_strip(sweep, first, last, mirrored=False):
        a, b = (s0, s1) if sweep % 2 == 0 else (s1, s0)
        copper_sweep(a, rs if sweep == 0 else b, rs, first, last, sweep, mirrored)

    def sweep_inner(sweep):
        sweep_main(sweep, SWEEPS + 1 + sweep, ROWS + SWEEPS - 1 - sweep)

    for sweep in range(2):
        sweep_inner(sweep)

    for c in t_halos:
        c.wait_recv()

    @pl.when(is_bottom)
    def _():
        for c in surfaces + planes:
            c.wait_recv()
        sub = sub_of((ROWS, LANES))
        lane = lane_of((ROWS, LANES))
        face_temp = route(surface[...].reshape(streams * ROWS, LANES), shift_ref[...] + i * ROWS, ROWS)
        t0 = n_send[3]
        t1 = tb[pl.ds(CELLS + 1, ROWS, stride=CELLS), :]
        v0 = n_send[2]
        mask = mask_ref[...]
        behind = jnp.where(sub == 0, jnp.broadcast_to(tb[pl.ds(0, 1), :], (ROWS, LANES)), roll(t0, 1, 0))
        ahead = jnp.where(
            sub == ROWS - 1,
            jnp.broadcast_to(tb[pl.ds((ROWS + 1) * CELLS, 1), :], (ROWS, LANES)),
            roll(t0, ROWS - 1, 0),
        )
        west = jnp.where(lane == 0, roll(t0_recv[0], 1), roll(t0, 1))
        east = jnp.where(lane == LANES - 1, roll(t0_recv[1], LANES - 1), roll(t0, LANES - 1))
        under = jnp.where(mask > 0, face_temp, t0)
        lap = (ahead + behind) + (west + east) + (under + t1) - 6.0 * t0
        grad = (ahead - behind) * 0.5
        new = t0 + DIFFUSIVITY * lap - ADVECTION * v0 * grad
        flux[i] = mask.astype(jnp.float32) * TRANSFER * (new - face_temp)
        for c in fluxes:
            c.start()
        for c in c_halos:
            c.start()
        below[0] = -v0
        below[1] = under

    for sweep in range(2, SWEEPS):
        sweep_inner(sweep)

    n_halos[0].wait_recv()

    @pl.when(jnp.logical_not(is_bottom))
    def _():
        below[0] = n_recv[0]
        below[1] = n_recv[1]

    for c in v_halos + w_halos + n_halos[1:]:
        c.wait_recv()

    sub32 = sub_of((CELLS, LANES))
    w_all = jnp.where((lane32 & 1) == 0, roll(w_recv[0], 1), roll(w_recv[1], LANES - 1))

    def fluid(row, carry):
        base = pl.multiple_of(row * CELLS, CELLS)
        here = pl.ds(base + CELLS, CELLS)
        velocity = vb[here, :]
        for field, (ref, out, coef) in enumerate(((vb, ov, VISCOSITY), (tb, ot, DIFFUSIVITY))):
            x = velocity if field == 0 else ref[here, :]
            behind = ref[pl.ds(base, CELLS), :]
            ahead = ref[pl.ds(base + 2 * CELLS, CELLS), :]
            ends = roll(w_all, lax.rem(LANES - 2 * row, LANES) if field == 0 else 64 - 2 * row)
            west = jnp.where(lane32 == 0, ends, roll(x, 1))
            east = jnp.where(lane32 == LANES - 1, ends, roll(x, LANES - 1))
            under = jnp.broadcast_to(below[field, pl.ds(row, 1), :], (CELLS, LANES))
            over = jnp.where(is_top, x[CELLS - 1 :], n_recv[2 + field, pl.ds(row, 1), :])
            over = jnp.broadcast_to(over, (CELLS, LANES))
            lower = jnp.where(sub32 == 0, under, roll(x, 1, 0))
            upper = jnp.where(sub32 == CELLS - 1, over, roll(x, CELLS - 1, 0))
            lap = (ahead + behind) + (west + east) + (lower + upper) - 6.0 * x
            grad = (ahead - behind) * 0.5
            out[pl.ds(base, CELLS), :] = x + coef * lap - ADVECTION * velocity * grad
        return carry

    rows_loop(0, ROWS, 8, fluid, 0)

    store_v = local(ov, v_out, 5)
    store_t = local(ot, t_out, 6)
    store_v.start()
    store_t.start()

    @pl.when(is_bottom)
    def _():
        for c in fluxes:
            c.wait_recv()
        amount = i * ROWS - SWEEPS - shift_ref[...]
        source[0] = route(flux[...].reshape(streams * ROWS, LANES), amount, SOURCE_ROWS)
        for c in copies + s_halos:
            c.start()

    for c in e_halos:
        c.wait_recv()

    def build(row, carry):
        group, place = edge_index(row)
        east = roll(e_recv[1, group], lax.rem(LANES + 32 - place, LANES))
        west = roll(e_recv[0, group], 122 - place)
        rs[row] = jnp.where(part == 2, east, jnp.where(part == 3, west, rs[row]))
        return carry

    rows_loop(SWEEPS, STRIP, 4, build, 0)
    for sweep in range(SWEEPS):
        sweep_strip(sweep, SWEEPS + 1 + sweep, STRIP, True)

    for c in c_halos:
        c.wait_recv()
    rows_loop(0, SWEEPS, 6, arrange, 0)
    rows_loop(SWEEPS + ROWS, EXT, 6, arrange, 0)

    for c in corners:
        c.wait_recv()
    for side in range(2):
        ups, downs = corner_recv[2 * side], corner_recv[2 * side + 1]
        even = jnp.where(halves, ups, roll(downs, 64))
        odd = jnp.where(halves, roll(ups, 64), downs)
        e_recv[side, 2] = jnp.stack((even, odd), axis=1).reshape(8, 8, LANES)

    def begin_strip(row, carry):
        keep_own(row, ends_of(row, EXT - 1 - row))
        return build(row, carry)

    rows_loop(0, SWEEPS, 6, begin_strip, 0)
    for sweep in range(SWEEPS):
        sweep_main(sweep, 1 + sweep, SWEEPS + 1 + sweep)
        sweep_main(sweep, ROWS + SWEEPS - 1 - sweep, EXT - 1 - sweep)
        sweep_strip(sweep, 1 + sweep, SWEEPS + 1 + sweep)
        if sweep == 3:
            for m in range(1, depths):

                @pl.when(k == m)
                def _():
                    copies[m - 1].wait_recv()
                    for c in s_halos:
                        c.start()


    for n in range(HALF):
        up, down = pl.ds(n, 1), pl.ds(ROWS - 1 - n, 1)
        main_top[up, :] = x1[n + SWEEPS, 0, pl.ds(0, 1), :]
        main_top[down, :] = x1[EXT - 1 - SWEEPS - n, 0, pl.ds(0, 1), :]
        strip_top[up, :] = s1[n + SWEEPS, 0, pl.ds(0, 1), :]
        strip_top[down, :] = s1[n + SWEEPS, 0, pl.ds(0, 1), :]
    for n, plane in enumerate(response(source[0])):
        main_part[n] = plane

    lane1 = lane_of((8, LANES))

    for c in s_halos:
        c.wait_recv()

    def turn(row, carry):
        for side in range(3):
            turned[side, pl.ds(row, 1), :] = source[side, pl.ds(EXT - 1 - row, 1), :]
        return carry

    rows_loop(0, ROWS, 8, turn, 0)
    straight = pl.ds(0, ROWS)
    strip_source = regions(
        lane32,
        (
            source[0, straight, :],
            roll(source[0, straight, :], 32),
            roll(source[2, straight, :], 32),
            roll(turned[1], 64),
            roll(turned[0], 64),
            roll(turned[0], 96),
            roll(turned[2], 96),
            source[1, straight, :],
        ),
    )
    for n, plane in enumerate(response(strip_source)):
        strip_part[n] = plane

    def turn_part(n):
        strip_turned[n, pl.ds(0, HALF), :] = strip_part[n, pl.ds(SWEEPS, HALF), :]
        for row in range(HALF):
            strip_turned[n, pl.ds(ROWS - 1 - row, 1), :] = strip_part[n, pl.ds(SWEEPS + row, 1), :]

    turn_part(0)
    inner = pl.ds(SWEEPS, ROWS)

    columns = LANES // depths
    tiles = ROWS // 8
    new_surface = with_edges(main_top[...] + main_part[0, inner, :], strip_top[...] + strip_turned[0])
    packed = jnp.zeros((8, LANES), jnp.float32)
    width = LANES // tiles
    for t in range(tiles):
        moved = roll(new_surface[8 * t : 8 * t + 8], lax.rem(LANES + width * t - columns * k, LANES))
        packed = jnp.where(lane1 // width == t, moved, packed)
    wall_send[...] = packed
    for c in walls:
        c.start()
    wall_all[i] = packed
    shift = roll(jnp.broadcast_to(shift_ref[...], (8, LANES)), lax.rem(LANES - columns * k, LANES))[:1]
    def assemble(n, carry):
        low, high = n, ROWS - 1 - n
        strip = s1[n + SWEEPS]
        right = roll(strip, 96)
        other = roll(jnp.where(lane8 < 64, right, strip), 64)
        for row, left, end in ((low, strip, right), (high, other, other)):
            main = x1[row + SWEEPS]
            done = jnp.where(lane8 < SWEEPS, left, jnp.where(lane8 >= LANES - SWEEPS, end, main))
            for r in range(8):
                oc[pl.ds(row * LAYERS + r, 8, stride=8), :] = done[r]
        return carry

    rows_loop(0, HALF, 4, assemble, 0)
    for n in range(SWEEPS):
        if n > 0:
            turn_part(n)
        layer = pl.ds(n, ROWS, stride=LAYERS)
        oc[layer, :] += with_edges(main_part[n, inner, :], strip_turned[n])
    store_c = local(oc, c_out, 7)
    store_c.start()
    for c in walls:
        c.wait_recv()
    rows = [roll(wall_all[b], LANES - width * t) for b in range(streams) for t in range(tiles)]
    wall[...] = route(jnp.concatenate(rows, axis=0), shift + i * ROWS, ROWS)[:, :columns]
    store_wall = local(wall, wall_out, 8)
    store_wall.start()

    for c in t_halos + v_halos + w_halos + n_halos + c_halos + e_halos + corners + s_halos + walls:
        c.wait_send()

    @pl.when(is_bottom)
    def _():
        for c in surfaces + planes + fluxes + copies:
            c.wait_send()

    for c in (store_v, store_t, store_c, store_wall):
        c.wait()


def write_out(*refs):
    sources, results, stages = refs[:4], refs[4:8], refs[8:12]
    semaphores = refs[12]
    steps = []
    for source, result, stage in zip(sources, results, stages):
        rows = source.shape[0]
        parts = max(1, rows // 512)
        for part in range(parts):
            at = pl.ds(part * (rows // parts), rows // parts)
            read, write = semaphores.at[2 * len(steps)], semaphores.at[2 * len(steps) + 1]
            steps.append(
                (
                    pltpu.make_async_copy(source.at[at], stage.at[at], read),
                    pltpu.make_async_copy(stage.at[at], result.at[at], write),
                )
            )
    for read, _ in steps:
        read.start()
    for read, write in steps:
        read.wait()
        write.start()
    for _, write in steps:
        write.wait()


def per_device(fluid_velocity, fluid_temp, solid_temp, channel_mask, owner_shift):
    f32 = jnp.float32
    streams, depths = lax.axis_size("stream"), lax.axis_size("depth")
    fluid_rows, copper_rows = ROWS * CELLS, ROWS * LAYERS
    anywhere = pl.BlockSpec(memory_space=pl.ANY)
    messages = GATHER + 3 * streams + depths
    outs = pl.pallas_call(
        kernel,
        out_shape=(
            jax.ShapeDtypeStruct((fluid_rows, LANES), f32),
            jax.ShapeDtypeStruct((fluid_rows, LANES), f32),
            jax.ShapeDtypeStruct((copper_rows, LANES), f32),
            jax.ShapeDtypeStruct((ROWS, LANES // depths), f32),
        ),
        in_specs=[anywhere] * 5,
        out_specs=(anywhere,) * 4,
        scratch_shapes=[
            pltpu.VMEM(((ROWS + 2) * CELLS, LANES), f32),
            pltpu.VMEM(((ROWS + 2) * CELLS, LANES), f32),
            pltpu.VMEM((EXT * LAYERS, LANES), f32),
            *[pltpu.VMEM((EXT, 8, 8, LANES), f32)] * 3,
            *[pltpu.VMEM((STRIP, 8, 8, LANES), f32)] * 3,
            pltpu.VMEM((4, ROWS, LANES), f32),
            pltpu.VMEM((4, ROWS, LANES), f32),
            pltpu.VMEM((CELLS, LANES), f32),
            pltpu.VMEM((2, CELLS, LANES), f32),
            pltpu.VMEM((2, ROWS, LANES), f32),
            pltpu.VMEM((2, GROUPS - 1, 8, 8, LANES), f32),
            pltpu.VMEM((2, GROUPS, 8, 8, LANES), f32),
            pltpu.VMEM((streams, ROWS, LANES), f32),
            pltpu.VMEM((streams, ROWS, LANES), f32),
            pltpu.VMEM((3, SOURCE_ROWS, LANES), f32),
            pltpu.VMEM((8, LANES), f32),
            pltpu.VMEM((streams, 8, LANES), f32),
            pltpu.VMEM((2, ROWS, LANES), f32),
            pltpu.VMEM((ROWS, LANES), jnp.int32),
            pltpu.VMEM((1, LANES), jnp.int32),
            pltpu.VMEM((2, 2, 4, 8, LANES), f32),
            pltpu.VMEM((4, 4, 8, LANES), f32),
            pltpu.VMEM((fluid_rows, LANES), f32),
            pltpu.VMEM((fluid_rows, LANES), f32),
            pltpu.VMEM((copper_rows, LANES), f32),
            pltpu.VMEM((ROWS, LANES // depths), f32),
            pltpu.VMEM((SWEEPS, SOURCE_ROWS, LANES), f32),
            pltpu.VMEM((SWEEPS, ROWS, LANES), f32),
            pltpu.VMEM((SWEEPS, ROWS, LANES), f32),
            pltpu.VMEM((3, ROWS, LANES), f32),
            pltpu.VMEM((ROWS, LANES), f32),
            pltpu.VMEM((ROWS, LANES), f32),
            pltpu.SemaphoreType.DMA((messages,)),
            pltpu.SemaphoreType.DMA((messages,)),
            pltpu.SemaphoreType.DMA((9,)),
        ],
        compiler_params=pltpu.CompilerParams(
            collective_id=0, has_side_effects=True, vmem_limit_bytes=57 * 1024 * 1024
        ),
    )(
        fluid_velocity.reshape(fluid_rows, LANES),
        fluid_temp.reshape(fluid_rows, LANES),
        solid_temp.reshape(copper_rows, LANES),
        channel_mask,
        owner_shift.reshape(1, LANES),
    )
    outs = pl.pallas_call(
        write_out,
        out_shape=tuple(jax.ShapeDtypeStruct(o.shape, o.dtype) for o in outs),
        in_specs=[anywhere] * 4,
        out_specs=(anywhere,) * 4,
        scratch_shapes=[pltpu.VMEM(o.shape, o.dtype) for o in outs] + [pltpu.SemaphoreType.DMA((20,))],
        compiler_params=pltpu.CompilerParams(vmem_limit_bytes=57 * 1024 * 1024),
    )(*outs)
    return (
        outs[0].reshape(fluid_velocity.shape),
        outs[1].reshape(fluid_temp.shape),
        outs[2].reshape(solid_temp.shape),
        outs[3],
    )


def solution(mesh):
    placed = (
        P("stream", "depth", "span"),
        P("stream", "depth", "span"),
        P("stream", None, "span"),
        P("stream", "span"),
        P("span"),
    )
    return jax.shard_map(
        per_device,
        mesh=mesh,
        in_specs=placed,
        out_specs=(
            P("stream", "depth", "span"),
            P("stream", "depth", "span"),
            P("stream", None, "span"),
            P("stream", ("span", "depth")),
        ),
        check_vma=False,
    )
```

```python
import math

import jax
import jax.numpy as jnp
from jax import lax
from jax.experimental import pallas as pl
from jax.experimental.pallas import tpu as pltpu
from jax.sharding import PartitionSpec as P

SWEEPS = 6
VISCOSITY = 0.1
DIFFUSIVITY = 0.15
ADVECTION = 0.2
TRANSFER = 0.5

LANES = 128
ROWS = 32
CELLS = 32
LAYERS = 64
EXT = ROWS + 2 * SWEEPS
HALF = ROWS // 2
STRIP = HALF + SWEEPS
PACK = 10
GROUPS = 3
SOURCE_ROWS = 48

V_UP, V_DOWN, T_UP, T_DOWN = 0, 1, 2, 3
N_UP, N_DOWN = 4, 5
W_UP, W_DOWN = 6, 7
T0_UP, T0_DOWN = 8, 9
C_UP, C_DOWN = 10, 11
E_UP, E_DOWN = 12, 13
S_UP, S_DOWN = 14, 15
CORNER = 16
GATHER = 20


def weight(sweep):
    return 1.0 / (1.0 + 6.0 / 7.0 * math.cos(math.pi * (2 * sweep + 1) / (2 * SWEEPS)))


def lane_of(shape):
    return lax.broadcasted_iota(jnp.int32, shape, len(shape) - 1)


def sub_of(shape):
    return lax.broadcasted_iota(jnp.int32, shape, len(shape) - 2)


def roll(x, shift, axis=None):
    axis = x.ndim - 1 if axis is None else axis
    if isinstance(shift, int):
        shift = shift % x.shape[axis]
        if shift == 0:
            return x
    return pltpu.roll(x, shift, axis)


def route(plane, amount, wanted):
    total = plane.shape[0]
    amount = amount & (total - 1)
    step = total // 2
    plane = jnp.concatenate((plane, plane[:wanted]), axis=0)
    while step >= 8:
        keep = wanted + step
        bits = jnp.broadcast_to(amount, (keep, LANES)) & step
        plane = jnp.where(bits != 0, plane[step : step + keep], plane[:keep])
        step //= 2
    keep = wanted + 8
    while step >= 1:
        bits = jnp.broadcast_to(amount, (keep, LANES)) & step
        plane = jnp.where(bits != 0, roll(plane, keep - step, 0), plane)
        step //= 2
    return plane[:wanted]


def regions(lane, parts):
    out = parts[7]
    for n in range(6, -1, -1):
        out = jnp.where(lane < 16 * (n + 1), parts[n], out)
    return out


def rows_loop(first, last, unroll, body, carry):
    count = (last - first) // unroll

    def several(n, carry):
        for u in range(unroll):
            carry = body(first + n * unroll + u, carry)
        return carry

    carry = several(0, carry) if count == 1 else lax.fori_loop(0, count, several, carry)
    for row in range(first + count * unroll, last):
        carry = body(row, carry)
    return carry


def after(src, row, cur, last, mirrored):
    if mirrored and row == last - 1:
        return roll(cur, 64)
    return src[row + 1]


def copper_sweep(out, src, rhs, first, last, sweep, mirrored=False):
    omega = weight(sweep)
    keep, gain = 1.0 - omega, omega / 7.0
    sub = sub_of((1, 8, LANES))

    def body(row, carry):
        prev, cur = carry
        nxt = after(src, row, cur, last, mirrored)
        side = roll(cur, 1) + roll(cur, LANES - 1)
        up = jnp.concatenate(
            (cur[1:], jnp.where(sub == 7, 0.0, roll(cur[:1], 7, 1))), axis=0
        )
        down = jnp.concatenate(
            (jnp.where(sub == 0, cur[:1], roll(cur[7:], 1, 1)), cur[:7]), axis=0
        )
        near = (prev + nxt) + (up + down) + side
        out[row] = keep * cur + gain * (rhs[row] + near)
        return cur, nxt

    unroll = last - first if last - first <= 16 else (last - first) // 2
    rows_loop(first, last, unroll, body, (src[first - 1], src[first]))


def response(source):
    layers = [weight(0) / 7.0 * source]
    rows = source.shape[0]
    for sweep in range(1, SWEEPS):
        omega = weight(sweep)
        keep, gain = 1.0 - omega, omega / 7.0
        new = []
        for n in range(sweep + 1):
            if n == sweep:
                new.append(gain * layers[n - 1])
                continue
            cur = layers[n]
            near = (roll(cur, 1, 0) + roll(cur, rows - 1, 0)) + (roll(cur, 1) + roll(cur, LANES - 1))
            near += layers[n - 1] if n > 0 else cur + source
            if n + 1 < sweep:
                near += layers[n + 1]
            new.append(keep * cur + gain * near)
        layers = new
    return layers


def with_edges(main, strip):
    lane = lane_of(main.shape)
    first, second = strip[:HALF], strip[HALF:]
    low = jnp.concatenate((first, roll(second, 64)), axis=0)
    high = jnp.concatenate((roll(first, 96), roll(second, 32)), axis=0)
    return jnp.where(lane < SWEEPS, low, jnp.where(lane >= LANES - SWEEPS, high, main))


def edge_index(row):
    n = jnp.where(row < SWEEPS, 2 * PACK + row, row - SWEEPS)
    group = n // PACK
    return group, SWEEPS * (n - group * PACK)


def kernel(
    v_in,
    t_in,
    c_in,
    mask_in,
    shift_in,
    v_out,
    t_out,
    c_out,
    wall_out,
    vb,
    tb,
    xn,
    rm,
    x0,
    x1,
    rs,
    s0,
    s1,
    n_send,
    n_recv,
    w_send,
    w_recv,
    t0_recv,
    e_send,
    e_recv,
    surface,
    flux,
    source,
    wall_send,
    wall_all,
    below,
    mask_ref,
    shift_ref,
    corner_send,
    corner_recv,
    ov,
    ot,
    oc,
    wall,
    main_part,
    strip_part,
    strip_turned,
    turned,
    main_top,
    strip_top,
    send_sem,
    recv_sem,
    local_sem,
):
    streams, spans, depths = (lax.axis_size(a) for a in ("stream", "span", "depth"))
    i, j, k = (lax.axis_index(a) for a in ("stream", "span", "depth"))
    up_i, down_i = lax.rem(i + 1, streams), lax.rem(i + streams - 1, streams)
    up_j, down_j = lax.rem(j + 1, spans), lax.rem(j + spans - 1, spans)
    up_k, down_k = lax.rem(k + 1, depths), lax.rem(k + depths - 1, depths)
    is_bottom, is_top = k == 0, k == depths - 1
    mesh_id = pl.DeviceIdType.MESH

    def remote(src, dst, index, **where):
        return pltpu.make_async_remote_copy(
            src_ref=src,
            dst_ref=dst,
            send_sem=send_sem.at[index],
            recv_sem=recv_sem.at[index],
            device_id=where,
            device_id_type=mesh_id,
        )

    def local(src, dst, index):
        return pltpu.make_async_copy(src, dst, local_sem.at[index])

    barrier = pltpu.get_barrier_semaphore()
    for m in range(1, streams):
        pl.semaphore_signal(barrier, inc=1, device_id={"stream": lax.rem(i + m, streams)}, device_id_type=mesh_id)
    for other in (up_j, down_j):
        pl.semaphore_signal(barrier, inc=1, device_id={"span": other}, device_id_type=mesh_id)
    for a in (up_i, down_i):
        for b in (up_j, down_j):
            pl.semaphore_signal(barrier, inc=1, device_id={"stream": a, "span": b}, device_id_type=mesh_id)
    for m in range(1, depths):
        pl.semaphore_signal(barrier, inc=1, device_id={"depth": lax.rem(k + m, depths)}, device_id_type=mesh_id)

    load_t = local(t_in, tb.at[pl.ds(CELLS, ROWS * CELLS)], 0)
    load_v = local(v_in, vb.at[pl.ds(CELLS, ROWS * CELLS)], 1)
    load_c = local(c_in, xn.at[pl.ds(SWEEPS * LAYERS, ROWS * LAYERS)], 2)
    load_mask = local(mask_in, mask_ref, 3)
    load_shift = local(shift_in, shift_ref, 4)
    loads = (load_t, load_c, load_v, load_mask, load_shift)
    for c in loads:
        c.start()

    lane32 = lane_of((CELLS, LANES))
    load_t.wait()
    n_send[3] = tb[pl.ds(CELLS, ROWS, stride=CELLS), :]
    load_c.wait()
    surface[i] = xn[pl.ds(SWEEPS * LAYERS, ROWS, stride=LAYERS), :]
    pl.semaphore_wait(barrier, streams - 1 + 2 + 4 + depths - 1)

    surfaces = [
        remote(surface.at[i], surface.at[i], GATHER + m, stream=lax.rem(i + m, streams))
        for m in range(1, streams)
    ]
    fluxes = [
        remote(flux.at[i], flux.at[i], GATHER + streams + m, stream=lax.rem(i + m, streams))
        for m in range(1, streams)
    ]
    walls = [
        remote(wall_send, wall_all.at[i], GATHER + 2 * streams + m, stream=lax.rem(i + m, streams))
        for m in range(1, streams)
    ]
    planes = [
        remote(n_send.at[3], t0_recv.at[0], T0_UP, span=up_j),
        remote(n_send.at[3], t0_recv.at[1], T0_DOWN, span=down_j),
    ]
    last, first = pl.ds(ROWS * CELLS, CELLS), pl.ds(CELLS, CELLS)
    before, after = pl.ds(0, CELLS), pl.ds((ROWS + 1) * CELLS, CELLS)
    t_halos = [
        remote(tb.at[last], tb.at[before], T_UP, stream=up_i),
        remote(tb.at[first], tb.at[after], T_DOWN, stream=down_i),
    ]
    v_halos = [
        remote(vb.at[last], vb.at[before], V_UP, stream=up_i),
        remote(vb.at[first], vb.at[after], V_DOWN, stream=down_i),
    ]
    n_halos = [
        remote(n_send.at[pl.ds(0, 2)], n_recv.at[pl.ds(0, 2)], N_UP, depth=up_k),
        remote(n_send.at[pl.ds(2, 2)], n_recv.at[pl.ds(2, 2)], N_DOWN, depth=down_k),
    ]
    w_halos = [
        remote(w_send, w_recv.at[0], W_UP, span=up_j),
        remote(w_send, w_recv.at[1], W_DOWN, span=down_j),
    ]
    wide = SWEEPS * LAYERS
    c_halos = [
        remote(xn.at[pl.ds(ROWS * LAYERS, wide)], xn.at[pl.ds(0, wide)], C_UP, stream=up_i),
        remote(xn.at[pl.ds(wide, wide)], xn.at[pl.ds(wide + ROWS * LAYERS, wide)], C_DOWN, stream=down_i),
    ]
    e_halos = [
        remote(e_send.at[0], e_recv.at[0, pl.ds(0, 2)], E_UP, span=up_j),
        remote(e_send.at[1], e_recv.at[1, pl.ds(0, 2)], E_DOWN, span=down_j),
    ]
    corners = [
        remote(corner_send.at[0, 0], corner_recv.at[0], CORNER, stream=up_i, span=up_j),
        remote(corner_send.at[0, 1], corner_recv.at[1], CORNER + 1, stream=down_i, span=up_j),
        remote(corner_send.at[1, 0], corner_recv.at[2], CORNER + 2, stream=up_i, span=down_j),
        remote(corner_send.at[1, 1], corner_recv.at[3], CORNER + 3, stream=down_i, span=down_j),
    ]
    s_halos = [
        remote(source.at[0], source.at[1], S_UP, span=up_j),
        remote(source.at[0], source.at[2], S_DOWN, span=down_j),
    ]
    copies = [
        remote(source.at[0], source.at[0], GATHER + 3 * streams + m, depth=m) for m in range(1, depths)
    ]

    @pl.when(is_bottom)
    def _():
        for c in surfaces + planes:
            c.start()

    for c in t_halos:
        c.start()

    @pl.when(jnp.logical_not(is_bottom))
    def _():
        for c in c_halos:
            c.start()

    n_send[1] = tb[pl.ds(CELLS + CELLS - 1, ROWS, stride=CELLS), :]
    load_v.wait()
    n_send[0] = vb[pl.ds(CELLS + CELLS - 1, ROWS, stride=CELLS), :]
    n_send[2] = vb[pl.ds(CELLS, ROWS, stride=CELLS), :]
    load_mask.wait()
    load_shift.wait()
    for c in v_halos + n_halos:
        c.start()

    def pack_fluid(row, packed):
        at = pl.ds(pl.multiple_of(CELLS + row * CELLS, CELLS), CELLS)
        low = 2 * row
        for ref, place in ((vb, low), (tb, low + 64)):
            chosen = jnp.logical_or(lane32 == place, lane32 == ((place + LANES - 1) & (LANES - 1)))
            packed = jnp.where(chosen, roll(ref[at, :], place), packed)
        return packed

    w_send[...] = rows_loop(0, ROWS, 8, pack_fluid, jnp.zeros((CELLS, LANES), jnp.float32))

    for c in w_halos:
        c.start()

    def arrange(row, carry):
        base = row * LAYERS
        for r in range(8):
            rm[row, r] = xn[pl.ds(base + r, 8, stride=8), :]
        return carry

    rows_loop(SWEEPS, SWEEPS + ROWS, 4, arrange, 0)

    lane8 = lane_of((8, 8, LANES))
    part = (lane8 & 63) // 16
    outer = jnp.logical_or(lane8 < 32, lane8 >= 96)

    def ends_of(row, other):
        return jnp.where(outer, rm[row], roll(rm[other], 64))

    def keep_own(row, ends):
        rs[row] = jnp.where(part == 1, roll(ends, 32), ends)

    def pack(ends, place, carry):
        high, low = carry
        chosen = jnp.logical_and((lane8 & 63) >= place, (lane8 & 63) < place + SWEEPS)
        return (
            jnp.where(chosen, roll(ends, place + SWEEPS), high),
            jnp.where(chosen, roll(ends, place), low),
        )

    zero8 = jnp.zeros((8, 8, LANES), jnp.float32)

    def pack_corner(n, carry):
        return pack(ends_of(ROWS + n, 2 * SWEEPS - 1 - n), SWEEPS * n, carry)

    halves = lane_of((4, 8, LANES)) < 64
    for side, both in enumerate(rows_loop(0, SWEEPS, 3, pack_corner, (zero8, zero8))):
        folded = both.reshape(4, 2, 8, LANES)
        even, odd = folded[:, 0], folded[:, 1]
        corner_send[side, 0] = jnp.where(halves, even, roll(odd, 64))
        corner_send[side, 1] = jnp.where(halves, roll(even, 64), odd)
    for group, count in enumerate((PACK, STRIP - SWEEPS - PACK)):

        def pack_own(n, carry):
            row = SWEEPS + group * PACK + n
            ends = ends_of(row, EXT - 1 - row)
            keep_own(row, ends)
            return pack(ends, SWEEPS * n, carry)

        e_send[0, group], e_send[1, group] = rows_loop(0, count, 2, pack_own, (zero8, zero8))

    for c in e_halos + corners:
        c.start()


    def sweep_main(sweep, first, last):
        a, b = (x0, x1) if sweep % 2 == 0 else (x1, x0)
        copper_sweep(a, rm if sweep == 0 else b, rm, first, last, sweep)

    def sweep_strip(sweep, first, last, mirrored=False):
        a, b = (s0, s1) if sweep % 2 == 0 else (s1, s0)
        copper_sweep(a, rs if sweep == 0 else b, rs, first, last, sweep, mirrored)

    def sweep_inner(sweep):
        sweep_main(sweep, SWEEPS + 1 + sweep, ROWS + SWEEPS - 1 - sweep)

    for sweep in range(2):
        sweep_inner(sweep)

    for c in t_halos:
        c.wait_recv()

    @pl.when(is_bottom)
    def _():
        for c in surfaces + planes:
            c.wait_recv()
        sub = sub_of((ROWS, LANES))
        lane = lane_of((ROWS, LANES))
        face_temp = route(surface[...].reshape(streams * ROWS, LANES), shift_ref[...] + i * ROWS, ROWS)
        t0 = n_send[3]
        t1 = tb[pl.ds(CELLS + 1, ROWS, stride=CELLS), :]
        v0 = n_send[2]
        mask = mask_ref[...]
        behind = jnp.where(sub == 0, jnp.broadcast_to(tb[pl.ds(0, 1), :], (ROWS, LANES)), roll(t0, 1, 0))
        ahead = jnp.where(
            sub == ROWS - 1,
            jnp.broadcast_to(tb[pl.ds((ROWS + 1) * CELLS, 1), :], (ROWS, LANES)),
            roll(t0, ROWS - 1, 0),
        )
        west = jnp.where(lane == 0, roll(t0_recv[0], 1), roll(t0, 1))
        east = jnp.where(lane == LANES - 1, roll(t0_recv[1], LANES - 1), roll(t0, LANES - 1))
        under = jnp.where(mask > 0, face_temp, t0)
        lap = (ahead + behind) + (west + east) + (under + t1) - 6.0 * t0
        grad = (ahead - behind) * 0.5
        new = t0 + DIFFUSIVITY * lap - ADVECTION * v0 * grad
        flux[i] = mask.astype(jnp.float32) * TRANSFER * (new - face_temp)
        for c in fluxes:
            c.start()
        for c in c_halos:
            c.start()
        below[0] = -v0
        below[1] = under

    for sweep in range(2, SWEEPS):
        sweep_inner(sweep)

    for c in e_halos:
        c.wait_recv()

    def build(row, carry):
        group, place = edge_index(row)
        east = roll(e_recv[1, group], lax.rem(LANES + 32 - place, LANES))
        west = roll(e_recv[0, group], 122 - place)
        rs[row] = jnp.where(part == 2, east, jnp.where(part == 3, west, rs[row]))
        return carry

    rows_loop(SWEEPS, STRIP, 4, build, 0)
    for sweep in range(SWEEPS):
        sweep_strip(sweep, SWEEPS + 1 + sweep, STRIP, True)
    @pl.when(is_bottom)
    def _():
        for c in fluxes:
            c.wait_recv()
        amount = i * ROWS - SWEEPS - shift_ref[...]
        source[0] = route(flux[...].reshape(streams * ROWS, LANES), amount, SOURCE_ROWS)
        for c in copies + s_halos:
            c.start()


    for c in c_halos:
        c.wait_recv()
    rows_loop(0, SWEEPS, 6, arrange, 0)
    rows_loop(SWEEPS + ROWS, EXT, 6, arrange, 0)

    for c in corners:
        c.wait_recv()
    for side in range(2):
        ups, downs = corner_recv[2 * side], corner_recv[2 * side + 1]
        even = jnp.where(halves, ups, roll(downs, 64))
        odd = jnp.where(halves, roll(ups, 64), downs)
        e_recv[side, 2] = jnp.stack((even, odd), axis=1).reshape(8, 8, LANES)

    def begin_strip(row, carry):
        keep_own(row, ends_of(row, EXT - 1 - row))
        return build(row, carry)

    rows_loop(0, SWEEPS, 6, begin_strip, 0)
    for sweep in range(SWEEPS):
        sweep_main(sweep, 1 + sweep, SWEEPS + 1 + sweep)
        sweep_main(sweep, ROWS + SWEEPS - 1 - sweep, EXT - 1 - sweep)
        sweep_strip(sweep, 1 + sweep, SWEEPS + 1 + sweep)
        if sweep == 3:
            for m in range(1, depths):

                @pl.when(k == m)
                def _():
                    copies[m - 1].wait_recv()
                    for c in s_halos:
                        c.start()


    for n in range(HALF):
        up, down = pl.ds(n, 1), pl.ds(ROWS - 1 - n, 1)
        main_top[up, :] = x1[n + SWEEPS, 0, pl.ds(0, 1), :]
        main_top[down, :] = x1[EXT - 1 - SWEEPS - n, 0, pl.ds(0, 1), :]
        strip_top[up, :] = s1[n + SWEEPS, 0, pl.ds(0, 1), :]
        strip_top[down, :] = s1[n + SWEEPS, 0, pl.ds(0, 1), :]
    for n, plane in enumerate(response(source[0])):
        main_part[n] = plane

    lane1 = lane_of((8, LANES))

    for c in s_halos:
        c.wait_recv()

    def turn(row, carry):
        for side in range(3):
            turned[side, pl.ds(row, 1), :] = source[side, pl.ds(EXT - 1 - row, 1), :]
        return carry

    rows_loop(0, ROWS, 8, turn, 0)
    straight = pl.ds(0, ROWS)
    strip_source = regions(
        lane32,
        (
            source[0, straight, :],
            roll(source[0, straight, :], 32),
            roll(source[2, straight, :], 32),
            roll(turned[1], 64),
            roll(turned[0], 64),
            roll(turned[0], 96),
            roll(turned[2], 96),
            source[1, straight, :],
        ),
    )
    for n, plane in enumerate(response(strip_source)):
        strip_part[n] = plane

    def turn_part(n):
        strip_turned[n, pl.ds(0, HALF), :] = strip_part[n, pl.ds(SWEEPS, HALF), :]
        for row in range(HALF):
            strip_turned[n, pl.ds(ROWS - 1 - row, 1), :] = strip_part[n, pl.ds(SWEEPS + row, 1), :]

    turn_part(0)
    inner = pl.ds(SWEEPS, ROWS)

    columns = LANES // depths
    tiles = ROWS // 8
    new_surface = with_edges(main_top[...] + main_part[0, inner, :], strip_top[...] + strip_turned[0])
    packed = jnp.zeros((8, LANES), jnp.float32)
    width = LANES // tiles
    for t in range(tiles):
        moved = roll(new_surface[8 * t : 8 * t + 8], lax.rem(LANES + width * t - columns * k, LANES))
        packed = jnp.where(lane1 // width == t, moved, packed)
    wall_send[...] = packed
    for c in walls:
        c.start()
    wall_all[i] = packed
    shift = roll(jnp.broadcast_to(shift_ref[...], (8, LANES)), lax.rem(LANES - columns * k, LANES))[:1]
    def assemble(n, carry):
        low, high = n, ROWS - 1 - n
        strip = s1[n + SWEEPS]
        right = roll(strip, 96)
        other = roll(jnp.where(lane8 < 64, right, strip), 64)
        for row, left, end in ((low, strip, right), (high, other, other)):
            main = x1[row + SWEEPS]
            done = jnp.where(lane8 < SWEEPS, left, jnp.where(lane8 >= LANES - SWEEPS, end, main))
            for r in range(8):
                oc[pl.ds(row * LAYERS + r, 8, stride=8), :] = done[r]
        return carry

    rows_loop(0, HALF, 4, assemble, 0)
    for n in range(SWEEPS):
        if n > 0:
            turn_part(n)
        layer = pl.ds(n, ROWS, stride=LAYERS)
        oc[layer, :] += with_edges(main_part[n, inner, :], strip_turned[n])
    store_c = local(oc, c_out, 7)
    store_c.start()

    n_halos[0].wait_recv()

    @pl.when(jnp.logical_not(is_bottom))
    def _():
        below[0] = n_recv[0]
        below[1] = n_recv[1]

    for c in v_halos + w_halos + n_halos[1:]:
        c.wait_recv()

    sub32 = sub_of((CELLS, LANES))
    w_all = jnp.where((lane32 & 1) == 0, roll(w_recv[0], 1), roll(w_recv[1], LANES - 1))

    def fluid(row, carry):
        base = pl.multiple_of(row * CELLS, CELLS)
        here = pl.ds(base + CELLS, CELLS)
        velocity = vb[here, :]
        for field, (ref, out, coef) in enumerate(((vb, ov, VISCOSITY), (tb, ot, DIFFUSIVITY))):
            x = velocity if field == 0 else ref[here, :]
            behind = ref[pl.ds(base, CELLS), :]
            ahead = ref[pl.ds(base + 2 * CELLS, CELLS), :]
            ends = roll(w_all, lax.rem(LANES - 2 * row, LANES) if field == 0 else 64 - 2 * row)
            west = jnp.where(lane32 == 0, ends, roll(x, 1))
            east = jnp.where(lane32 == LANES - 1, ends, roll(x, LANES - 1))
            under = jnp.broadcast_to(below[field, pl.ds(row, 1), :], (CELLS, LANES))
            over = jnp.where(is_top, x[CELLS - 1 :], n_recv[2 + field, pl.ds(row, 1), :])
            over = jnp.broadcast_to(over, (CELLS, LANES))
            lower = jnp.where(sub32 == 0, under, roll(x, 1, 0))
            upper = jnp.where(sub32 == CELLS - 1, over, roll(x, CELLS - 1, 0))
            lap = (ahead + behind) + (west + east) + (lower + upper) - 6.0 * x
            grad = (ahead - behind) * 0.5
            out[pl.ds(base, CELLS), :] = x + coef * lap - ADVECTION * velocity * grad
        return carry

    rows_loop(0, ROWS, 8, fluid, 0)

    store_v = local(ov, v_out, 5)
    store_t = local(ot, t_out, 6)
    store_v.start()
    store_t.start()

    for c in walls:
        c.wait_recv()
    rows = [roll(wall_all[b], LANES - width * t) for b in range(streams) for t in range(tiles)]
    wall[...] = route(jnp.concatenate(rows, axis=0), shift + i * ROWS, ROWS)[:, :columns]
    store_wall = local(wall, wall_out, 8)
    store_wall.start()

    for c in t_halos + v_halos + w_halos + n_halos + c_halos + e_halos + corners + s_halos + walls:
        c.wait_send()

    @pl.when(is_bottom)
    def _():
        for c in surfaces + planes + fluxes + copies:
            c.wait_send()

    for c in (store_v, store_t, store_c, store_wall):
        c.wait()


def write_out(*refs):
    sources, results, stages = refs[:4], refs[4:8], refs[8:12]
    semaphores = refs[12]
    steps = []
    for source, result, stage in zip(sources, results, stages):
        rows = source.shape[0]
        parts = max(1, rows // 512)
        for part in range(parts):
            at = pl.ds(part * (rows // parts), rows // parts)
            read, write = semaphores.at[2 * len(steps)], semaphores.at[2 * len(steps) + 1]
            steps.append(
                (
                    pltpu.make_async_copy(source.at[at], stage.at[at], read),
                    pltpu.make_async_copy(stage.at[at], result.at[at], write),
                )
            )
    for read, _ in steps:
        read.start()
    for read, write in steps:
        read.wait()
        write.start()
    for _, write in steps:
        write.wait()


def per_device(fluid_velocity, fluid_temp, solid_temp, channel_mask, owner_shift):
    f32 = jnp.float32
    streams, depths = lax.axis_size("stream"), lax.axis_size("depth")
    fluid_rows, copper_rows = ROWS * CELLS, ROWS * LAYERS
    anywhere = pl.BlockSpec(memory_space=pl.ANY)
    messages = GATHER + 3 * streams + depths
    outs = pl.pallas_call(
        kernel,
        out_shape=(
            jax.ShapeDtypeStruct((fluid_rows, LANES), f32),
            jax.ShapeDtypeStruct((fluid_rows, LANES), f32),
            jax.ShapeDtypeStruct((copper_rows, LANES), f32),
            jax.ShapeDtypeStruct((ROWS, LANES // depths), f32),
        ),
        in_specs=[anywhere] * 5,
        out_specs=(anywhere,) * 4,
        scratch_shapes=[
            pltpu.VMEM(((ROWS + 2) * CELLS, LANES), f32),
            pltpu.VMEM(((ROWS + 2) * CELLS, LANES), f32),
            pltpu.VMEM((EXT * LAYERS, LANES), f32),
            *[pltpu.VMEM((EXT, 8, 8, LANES), f32)] * 3,
            *[pltpu.VMEM((STRIP, 8, 8, LANES), f32)] * 3,
            pltpu.VMEM((4, ROWS, LANES), f32),
            pltpu.VMEM((4, ROWS, LANES), f32),
            pltpu.VMEM((CELLS, LANES), f32),
            pltpu.VMEM((2, CELLS, LANES), f32),
            pltpu.VMEM((2, ROWS, LANES), f32),
            pltpu.VMEM((2, GROUPS - 1, 8, 8, LANES), f32),
            pltpu.VMEM((2, GROUPS, 8, 8, LANES), f32),
            pltpu.VMEM((streams, ROWS, LANES), f32),
            pltpu.VMEM((streams, ROWS, LANES), f32),
            pltpu.VMEM((3, SOURCE_ROWS, LANES), f32),
            pltpu.VMEM((8, LANES), f32),
            pltpu.VMEM((streams, 8, LANES), f32),
            pltpu.VMEM((2, ROWS, LANES), f32),
            pltpu.VMEM((ROWS, LANES), jnp.int32),
            pltpu.VMEM((1, LANES), jnp.int32),
            pltpu.VMEM((2, 2, 4, 8, LANES), f32),
            pltpu.VMEM((4, 4, 8, LANES), f32),
            pltpu.VMEM((fluid_rows, LANES), f32),
            pltpu.VMEM((fluid_rows, LANES), f32),
            pltpu.VMEM((copper_rows, LANES), f32),
            pltpu.VMEM((ROWS, LANES // depths), f32),
            pltpu.VMEM((SWEEPS, SOURCE_ROWS, LANES), f32),
            pltpu.VMEM((SWEEPS, ROWS, LANES), f32),
            pltpu.VMEM((SWEEPS, ROWS, LANES), f32),
            pltpu.VMEM((3, ROWS, LANES), f32),
            pltpu.VMEM((ROWS, LANES), f32),
            pltpu.VMEM((ROWS, LANES), f32),
            pltpu.SemaphoreType.DMA((messages,)),
            pltpu.SemaphoreType.DMA((messages,)),
            pltpu.SemaphoreType.DMA((9,)),
        ],
        compiler_params=pltpu.CompilerParams(
            collective_id=0, has_side_effects=True, vmem_limit_bytes=57 * 1024 * 1024
        ),
    )(
        fluid_velocity.reshape(fluid_rows, LANES),
        fluid_temp.reshape(fluid_rows, LANES),
        solid_temp.reshape(copper_rows, LANES),
        channel_mask,
        owner_shift.reshape(1, LANES),
    )
    outs = pl.pallas_call(
        write_out,
        out_shape=tuple(jax.ShapeDtypeStruct(o.shape, o.dtype) for o in outs),
        in_specs=[anywhere] * 4,
        out_specs=(anywhere,) * 4,
        scratch_shapes=[pltpu.VMEM(o.shape, o.dtype) for o in outs] + [pltpu.SemaphoreType.DMA((20,))],
        compiler_params=pltpu.CompilerParams(vmem_limit_bytes=57 * 1024 * 1024),
    )(*outs)
    return (
        outs[0].reshape(fluid_velocity.shape),
        outs[1].reshape(fluid_temp.shape),
        outs[2].reshape(solid_temp.shape),
        outs[3],
    )


def solution(mesh):
    placed = (
        P("stream", "depth", "span"),
        P("stream", "depth", "span"),
        P("stream", None, "span"),
        P("stream", "span"),
        P("span"),
    )
    return jax.shard_map(
        per_device,
        mesh=mesh,
        in_specs=placed,
        out_specs=(
            P("stream", "depth", "span"),
            P("stream", "depth", "span"),
            P("stream", None, "span"),
            P("stream", ("span", "depth")),
        ),
        check_vma=False,
    )
```
